32 devices in a mesh: px: 8 (over z, x), py: 4 (over y, core).
Axes of the slice: x: 2, y: 2, z: 4, core: 2. Of those that a mesh axis runs over, the one named last changes fastest.
Arguments:
- counts: int32 [8], replicated, may hold values from 1 to 6, 16 in all
- coefficient: float32 [48, 4, 4096], P('px', 'py'), may hold values from 0.2 to 5
- signs: int32 [48, 4, 4096], P('px', 'py'), may hold values from 0 to 1
- basis_old: float32 [48, 4, 16, 4096], P('px', 'py'), may hold values from -8 to 8
- basis_last: float32 [48, 4, 16, 4096], P('px', 'py'), may hold values from -8 to 8
- residual_factor: float32 [16, 16], replicated, may hold values from -12 to 12
- previous_coef: float32 [32, 16], replicated, may hold values from -12 to 12
- sample_rows: int32 [2048], replicated, may hold values from 0 to 262143, as said below
Outputs:
- new_block: float32 [48, 4, 16, 4096], P('px', 'py')
- sketch: float32 [48, 2048], P(None, ('px', 'py'))
- solution: float32 [32, 16], replicated
The draws below stay inside these ranges and needn't reach their ends.
Inputs may be any that keep to these rules, and one draw needn't show every extreme that they name: Index i of px owns counts[i] consecutive patch columns, in px order; the largest count is exactly 6. `sample_rows`: distinct cell numbers, among them 0 and 262143.
All inputs are finite; a program needn't handle non-finite values.
Results may differ from the reference program's by a relative error of at most 0.0003.
Values sent between devices are 32-bit elements; how exact they have to be, the bound alone decides.
A program may use at most 256 MiB of HBM per device.

```python
import math
import jax
import jax.numpy as jnp
import numpy as np
from jax import lax

PS = 16
RHS = 16
K = 2048
MEANX = 2
CAP = 6
CELLS = 4096
GX = 16
NPATCH = 64
NC = 262144
N_PX = 8
N_PY = 4


def basis_pair(key):
    shape_all = (N_PX * CAP, N_PY, RHS, CELLS)
    fresh_old = jax.random.normal(jax.random.fold_in(key, 11), shape_all, jnp.float32)
    fresh_last = jax.random.normal(jax.random.fold_in(key, 12), shape_all, jnp.float32)
    mixing = jax.random.normal(jax.random.fold_in(key, 13), (RHS, RHS), jnp.float32) / math.sqrt(RHS)
    mixed = jnp.einsum('sygc,gh->syhc', fresh_last, mixing)
    older = 0.6 * mixed + 0.8 * fresh_old
    return (jnp.clip(older, -8.0, 8.0), jnp.clip(fresh_last, -8.0, 8.0))


def draw_basis_old(key, part):
    return basis_pair(key)[0]


def draw_basis_last(key, part):
    return basis_pair(key)[1]


def draw_previous_coef(key, part):
    noise = jnp.clip(jax.random.normal(jax.random.fold_in(key, 32), (2 * RHS, RHS), jnp.float32), -4.0, 4.0)
    leading = jnp.concatenate([6.0 * jnp.eye(RHS, dtype=jnp.float32), jnp.zeros((RHS, RHS), jnp.float32)], axis=0)
    return jnp.clip(leading + noise, -12.0, 12.0)


def draw_sample_rows(key, part):
    middle = jax.random.permutation(jax.random.fold_in(key, 21), NC - 2)[:K - 2].astype(jnp.int32) + 1
    chosen = jnp.concatenate([jnp.array([0, NC - 1], jnp.int32), middle])
    shuffle_idx = jax.random.permutation(jax.random.fold_in(key, 22), K)
    return chosen[shuffle_idx].astype(jnp.int32)


def touch_ends(values, own_key, low, top_value):
    dims = values.shape
    place = [jax.random.randint(jax.random.fold_in(own_key, axis), (), 0, dims[axis]) for axis in range(len(dims))]
    values = values.at[tuple(place)].set(low)
    longest = dims.index(max(dims))
    place[longest] = (place[longest] + 1) % dims[longest]
    return values.at[tuple(place)].set(top_value)


def steps_of(stream_key, shape, cuts, low, high):
    level = 1.0
    for position, blocks in cuts:
        steps = jax.random.uniform(jax.random.fold_in(jax.random.fold_in(stream_key, 6), position), (blocks,), jnp.float32, low / len(cuts), high / len(cuts))
        level = level * jnp.repeat(jnp.exp(steps), shape[position] // blocks).reshape((-1,) + (1,) * (len(shape) - 1 - position))
    return level


def length_profile(count, total, limit, skew):
    portions = [(1 << 20) // math.isqrt(grade ** skew) + 1 for grade in range(2, count + 1)]
    spare, holding = total - limit - (count - 1), [1] * (count - 1)
    while spare > 0:
        candidates = [i for i in range(count - 1) if holding[i] < limit]
        pool, budget = sum([portions[i] for i in candidates]), spare
        for i in candidates:
            extra = min(limit - holding[i], max(1, budget * portions[i] // pool), spare)
            holding[i] = holding[i] + extra
            spare = spare - extra
    return np.array([limit] + holding)


def uneven(own_key, count, total, reach, skew):
    if count == 2:
        one = jax.random.randint(own_key, (), max(1, total - reach), min(reach, total - 1) + 1)
        return jnp.stack([one, total - one])
    sizes = jnp.asarray(length_profile(count, total, reach, skew), jnp.int32)
    twos = (count - 1) // 2
    source_of, receiver = sizes[1:1 + 2 * twos:2], sizes[2:2 + 2 * twos:2]
    slack = jnp.minimum(source_of - 1, reach - receiver)
    passed = jax.random.randint(jax.random.fold_in(own_key, 1), (twos,), 0, 1 << 20) % (slack + 1)
    sizes = sizes.at[1:1 + 2 * twos:2].set(source_of - passed).at[2:2 + 2 * twos:2].set(receiver + passed)
    return sizes[jax.random.permutation(jax.random.fold_in(own_key, 2), count)]


def centred(own_key, dims, scale, bound, kind=jnp.bfloat16):
    drawn = scale * jax.random.normal(own_key, dims, jnp.float32)
    return jnp.clip(drawn, min=-bound, max=bound).astype(kind)


def setup_inputs(seed: int = 0) -> dict:
    arg_keys = jax.random.split(jax.random.key(seed), 9)
    counts = uneven(arg_keys[0], N_PX, MEANX * N_PX, 3 * MEANX, 2).astype(jnp.int32)
    coefficient = jnp.clip(jnp.exp(math.log(5.0) - 3.218876 * jax.random.uniform(arg_keys[1], (N_PX * CAP, N_PY, CELLS), jnp.float32) ** steps_of(arg_keys[1], (N_PX * CAP, N_PY, CELLS), ((0, 8), (1, 4)), -0.2, 0.2)), 0.2, 5.0)
    signs = touch_ends(jax.random.randint(arg_keys[2], (N_PX * CAP, N_PY, CELLS), 0, 2), jax.random.fold_in(arg_keys[2], 1), 0, 1).astype(jnp.int32)
    basis_old = draw_basis_old(jax.random.fold_in(arg_keys[8], 71), 0)
    basis_last = draw_basis_last(jax.random.fold_in(arg_keys[8], 71), 0)
    residual_factor = centred(arg_keys[5], (RHS, RHS), 3.0, 12.0, jnp.float32)
    previous_coef = draw_previous_coef(jax.random.fold_in(arg_keys[8], 71), 0)
    sample_rows = draw_sample_rows(jax.random.fold_in(arg_keys[8], 71), 0)
    return dict(counts=counts, coefficient=coefficient, signs=signs, basis_old=basis_old, basis_last=basis_last, residual_factor=residual_factor, previous_coef=previous_coef, sample_rows=sample_rows)


highest = lax.Precision.HIGHEST

def parity_of(values):
    folded = values
    for amount in (16, 8, 4, 2, 1):
        folded = jnp.bitwise_xor(folded, jnp.right_shift(folded, amount))
    return jnp.bitwise_and(folded, 1)

def sign_table(length):
    indices = jnp.arange(length, dtype=jnp.int32)
    parity = parity_of(jnp.bitwise_and(indices[:, None], indices[None, :]))
    return (1 - 2 * parity).astype(jnp.float32)

def transform_cells(values):
    inner_len = min(CELLS, 128)
    outer_len = CELLS // inner_len
    shaped = values.reshape(values.shape[:-1] + (outer_len, inner_len))
    shaped = jnp.einsum('sjab,bd->sjad', shaped, sign_table(inner_len), precision=highest)
    shaped = jnp.einsum('ca,sjad->sjcd', sign_table(outer_len), shaped, precision=highest)
    return shaped.reshape(values.shape)

def patch_slots(counts):
    offsets = jnp.cumsum(counts) - counts
    ends = offsets + counts
    column_ids = jnp.arange(GX, dtype=jnp.int32)
    owner_ids = lax.optimization_barrier(jnp.sum((column_ids[:, None] >= ends[None, :]).astype(jnp.int32), axis=1)).astype(jnp.int32)
    return (owner_ids * CAP + column_ids - offsets[owner_ids]).astype(jnp.int32)

def to_grid(field_vals):
    channels = field_vals.shape[2]
    cube_vals = field_vals.reshape(GX, N_PY, channels, PS, PS, PS)
    return jnp.transpose(cube_vals, (2, 0, 3, 1, 4, 5)).reshape(channels, GX * PS, N_PY * PS, PS)

def from_grid(grid_vals):
    channels = grid_vals.shape[0]
    cube_vals = grid_vals.reshape(channels, GX, PS, N_PY, PS, PS)
    return jnp.transpose(cube_vals, (1, 3, 0, 2, 4, 5)).reshape(GX, N_PY, channels, CELLS)

def operate_one(values, kappa_grid):
    padded = jnp.pad(values, 1)
    kappa_pad = jnp.pad(kappa_grid, 1)
    extents = values.shape
    summed = jnp.zeros_like(values)
    for movement in ((1, 0, 0), (-1, 0, 0), (0, 1, 0), (0, -1, 0), (0, 0, 1), (0, 0, -1)):
        starts = tuple((1 + movement[dim_idx] for dim_idx in range(3)))
        limits = tuple((starts[dim_idx] + extents[dim_idx] for dim_idx in range(3)))
        neighbour_vals = lax.slice(padded, starts, limits)
        neighbour_kappa = lax.slice(kappa_pad, starts, limits)
        summed = summed + 0.5 * (kappa_grid + neighbour_kappa) * (values - neighbour_vals)
    return summed

def sketch_rows(field_vals, sign_flips, sample_rows):
    columns = (field_vals * sign_flips[:, :, None, :]).reshape(NPATCH, field_vals.shape[2], CELLS)
    spread = transform_cells(columns)
    patch_ids = jnp.arange(NPATCH, dtype=jnp.int32)
    block_len = min(K, 512)
    row_blocks = sample_rows.reshape(K // block_len, block_len)

    def one_block(block_rows):
        picked = jnp.take(spread, block_rows % CELLS, axis=2)
        parity = parity_of(jnp.bitwise_and(patch_ids[:, None], (block_rows // CELLS)[None, :]))
        weights = (1 - 2 * parity).astype(jnp.float32)
        return jnp.einsum('pk,pjk->jk', weights, picked, precision=highest)
    pieces = lax.map(one_block, row_blocks)
    joined = jnp.transpose(pieces, (1, 0, 2)).reshape(field_vals.shape[2], K)
    return joined * (1.0 / math.sqrt(NC))

def normal_parts(sketch_cols, proj_coef, previous_coef, residual_factor):
    pair_count = proj_coef.shape[0]
    width_rhs = proj_coef.shape[1]
    pair_rows = sketch_cols[:pair_count]
    first_image = jnp.einsum('ab,ak->bk', previous_coef, pair_rows, precision=highest)
    second_image = jnp.einsum('ab,ak->bk', proj_coef, pair_rows, precision=highest) + sketch_cols[pair_count:]
    images = jnp.concatenate([first_image, second_image], axis=0)
    target = jnp.einsum('ab,ak->bk', residual_factor, sketch_cols[:width_rhs], precision=highest)
    return (jnp.dot(images, images.T, precision=highest), jnp.dot(images, target.T, precision=highest))

def solve_normal(normal_gram, normal_cross):
    factor_low = jnp.linalg.cholesky(normal_gram)
    middle = lax.linalg.triangular_solve(factor_low, normal_cross, left_side=True, lower=True)
    return lax.linalg.triangular_solve(factor_low, middle, left_side=True, lower=True, transpose_a=True)

def reference(counts, coefficient, signs, basis_old, basis_last, residual_factor, previous_coef, sample_rows):
    slot_ids = patch_slots(counts)
    old_glob = basis_old[slot_ids]
    last_glob = basis_last[slot_ids]
    kappa_glob = coefficient[slot_ids]
    sign_flips = (1 - 2 * signs[slot_ids]).astype(jnp.float32)
    kappa_grid = to_grid(kappa_glob[:, :, None, :])[0]
    image = from_grid(lax.map(lambda values: operate_one(values, kappa_grid), to_grid(last_glob)))
    pair = jnp.concatenate([old_glob, last_glob], axis=2)
    proj_coef = jnp.einsum('pyac,pybc->ab', pair, image, precision=highest) / NC
    newer = image - jnp.einsum('pyac,ab->pybc', pair, proj_coef, precision=highest)
    sketch = jnp.concatenate([sketch_rows(old_glob, sign_flips, sample_rows), sketch_rows(last_glob, sign_flips, sample_rows), sketch_rows(newer, sign_flips, sample_rows)], axis=0)
    normal_gram, normal_cross = normal_parts(sketch, proj_coef, previous_coef, residual_factor)
    solution = solve_normal(normal_gram, normal_cross)
    new_block = jnp.zeros((N_PX * CAP, N_PY, RHS, CELLS), jnp.float32).at[slot_ids].set(newer)
    return (new_block, sketch, solution)
```

```python
import functools
import math

import jax
import jax.numpy as jnp
from jax import lax
from jax.experimental import pallas as pl
from jax.experimental.pallas import tpu as pltpu
from jax.sharding import PartitionSpec as P

PS = 16
MEANX = 2
TILE = 256

highest = lax.Precision.HIGHEST
f32 = jnp.float32
bf16 = jnp.bfloat16
VMEM = pl.BlockSpec(memory_space=pltpu.VMEM)
SMEM = pl.BlockSpec(memory_space=pltpu.SMEM)


def params(**more):
    return pltpu.CompilerParams(vmem_limit_bytes=48 * 1024 * 1024, **more)


def parity_sign(values, bits):
    amount = 1
    while amount < bits:
        amount *= 2
    while amount > 1:
        amount //= 2
        values = jnp.bitwise_xor(values, jnp.right_shift(values, amount))
    return 1 - 2 * jnp.bitwise_and(values, 1)


def halo_kernel(
    n_px, n_py, counts_ref, last_ref, kap_ref, yg_ref, xg_ref, ybuf, xbuf, ysend, yrecv, xsend, xrecv
):
    i = lax.axis_index("px")
    j = lax.axis_index("py")
    cap = last_ref.shape[0]
    rhs = last_ref.shape[2]
    plane = PS * PS
    barrier = pltpu.get_barrier_semaphore()
    around = [
        ("py", j - 1, j > 0),
        ("py", j + 1, j < n_py - 1),
        ("px", i - 1, i > 0),
        ("px", i + 1, i < n_px - 1),
    ]
    for axis, index, valid in around:
        @pl.when(valid)
        def _(axis=axis, index=index):
            pl.semaphore_signal(
                barrier, inc=1, device_id={axis: index}, device_id_type=pl.DeviceIdType.MESH
            )

    lane = lax.broadcasted_iota(jnp.int32, (1, plane), 1)
    tail = jnp.clip(counts_ref[i] - 1, 0, cap - 1)
    xbuf[0, pl.ds(0, rhs), :] = last_ref[0, 0, :, pl.ds(0, plane)]
    xbuf[0, pl.ds(rhs, 1), :] = kap_ref[0, :, pl.ds(0, plane)]
    top = (PS - 1) * plane
    xbuf[1, pl.ds(0, rhs), :] = last_ref[tail, 0, :, pl.ds(top, plane)]
    xbuf[1, pl.ds(rhs, 1), :] = kap_ref[tail, :, pl.ds(top, plane)]

    def pack(s, carry):
        u0 = jnp.zeros((rhs, plane), f32)
        u1 = jnp.zeros((rhs, plane), f32)
        k0 = jnp.zeros((1, plane), f32)
        k1 = jnp.zeros((1, plane), f32)
        for a in range(PS):
            mine = lane // PS == a
            u = last_ref[s, 0, :, pl.ds(a * plane, plane)]
            k = kap_ref[s, :, pl.ds(a * plane, plane)]
            lo = (a * PS) % plane
            hi = (a * PS + PS) % plane
            u0 = jnp.where(mine, pltpu.roll(u, lo, 1) if lo else u, u0)
            u1 = jnp.where(mine, pltpu.roll(u, hi, 1) if hi else u, u1)
            k0 = jnp.where(mine, pltpu.roll(k, lo, 1) if lo else k, k0)
            k1 = jnp.where(mine, pltpu.roll(k, hi, 1) if hi else k, k1)
        ybuf[0, pl.ds(pl.multiple_of(s * rhs, 8), rhs), :] = u0
        ybuf[1, pl.ds(pl.multiple_of(s * rhs, 8), rhs), :] = u1
        ybuf[0, pl.ds(cap * rhs + s, 1), :] = k0
        ybuf[1, pl.ds(cap * rhs + s, 1), :] = k1
        return carry

    peers = sum(valid.astype(jnp.int32) for _, _, valid in around)
    pl.semaphore_wait(barrier, peers)

    def copy_of(base, side):
        axis, index, _ = around[base + side]
        buf, ghost, send, recv = (
            (xbuf, xg_ref, xsend, xrecv) if base == 2 else (ybuf, yg_ref, ysend, yrecv)
        )
        return pltpu.make_async_remote_copy(
            src_ref=buf.at[side],
            dst_ref=ghost.at[1 - side],
            send_sem=send.at[side],
            recv_sem=recv.at[1 - side],
            device_id={axis: index},
            device_id_type=pl.DeviceIdType.MESH,
        )

    for side in range(2):
        @pl.when(around[2 + side][2])
        def _(side=side):
            copy_of(2, side).start()

    lax.fori_loop(0, cap, pack, 0)

    for side in range(2):
        @pl.when(around[side][2])
        def _(side=side):
            copy_of(0, side).start()
    for base, ghost in ((0, yg_ref), (2, xg_ref)):
        for side in range(2):
            @pl.when(jnp.logical_not(around[base + side][2]))
            def _(ghost=ghost, side=side):
                ghost[side] = jnp.zeros(ghost.shape[1:], f32)
    for base in (2, 0):
        for side in range(2):
            @pl.when(around[base + side][2])
            def _(base=base, side=side):
                copy_of(base, side).wait_send()
    for base, ghost, buf, send, recv in (
        (2, xg_ref, xbuf, xsend, xrecv),
        (0, yg_ref, ybuf, ysend, yrecv),
    ):
        for side in range(2):
            axis, index, valid = around[base + side]

            @pl.when(valid)
            def _(ghost=ghost, buf=buf, side=side, send=send, recv=recv, axis=axis, index=index):
                pltpu.make_async_remote_copy(
                    src_ref=buf.at[side],
                    dst_ref=ghost.at[side],
                    send_sem=send.at[side],
                    recv_sem=recv.at[side],
                    device_id={axis: index},
                    device_id_type=pl.DeviceIdType.MESH,
                ).wait_recv()


def halo(n_px, n_py, counts, last, kap):
    cap, _, rhs, _ = last.shape
    plane = PS * PS
    yrows = cap * rhs + -(-cap // 8) * 8
    xrows = rhs + 8
    return pl.pallas_call(
        functools.partial(halo_kernel, n_px, n_py),
        out_shape=(
            jax.ShapeDtypeStruct((2, yrows, plane), f32),
            jax.ShapeDtypeStruct((2, xrows, plane), f32),
        ),
        in_specs=[SMEM, VMEM, VMEM],
        out_specs=(VMEM, VMEM),
        scratch_shapes=[
            pltpu.VMEM((2, yrows, plane), f32),
            pltpu.VMEM((2, xrows, plane), f32),
            pltpu.SemaphoreType.DMA((2,)),
            pltpu.SemaphoreType.DMA((2,)),
            pltpu.SemaphoreType.DMA((2,)),
            pltpu.SemaphoreType.DMA((2,)),
        ],
        compiler_params=params(collective_id=0, has_side_effects=True),
    )(counts, last, kap)


def split(values):
    head = values.astype(bf16)
    return head, (values - head.astype(f32)).astype(bf16)


def local_kernel(
    n_py, scale, counts_ref, last_ref, old_ref, kap_ref, sgn_ref, yg_ref, xg_ref, rows_ref,
    image_ref, gram_ref, sketch_ref, cols, table,
):
    i = lax.axis_index("px")
    j = lax.axis_index("py")
    cap, _, rhs, cells = last_ref.shape
    plane = PS * PS
    held = counts_ref[i]
    offset = lax.fori_loop(0, i, lambda t, acc: acc + counts_ref[t], jnp.int32(0))
    lane = lax.broadcasted_iota(jnp.int32, (1, plane), 1)
    b_id = lane // PS
    c_id = lane % PS
    top = (PS - 1) * plane

    def one_slot(s, carry):
        live = s < held
        first = s == 0
        final = s == held - 1
        before = jnp.maximum(s - 1, 0)
        after = jnp.minimum(s + 1, cap - 1)
        ks = pl.ds(cap * rhs + s, 1)
        us = pl.ds(pl.multiple_of(s * rhs, 8), rhs)
        kg_lo, kg_hi = yg_ref[0, ks, :], yg_ref[1, ks, :]
        ug_lo, ug_hi = yg_ref[0, us, :], yg_ref[1, us, :]
        for a in range(PS):
            at = pl.ds(a * plane, plane)

            def planes(ref_at, ghost_rows):
                if a == 0:
                    low = jnp.where(first, xg_ref[0, ghost_rows, :], ref_at(before, top))
                else:
                    low = ref_at(s, (a - 1) * plane)
                if a == PS - 1:
                    high = jnp.where(final, xg_ref[1, ghost_rows, :], ref_at(after, 0))
                else:
                    high = ref_at(s, (a + 1) * plane)
                return low, high

            def rolled(value, glo, ghi):
                lo = (plane - a * PS) % plane
                hi = (plane - PS - a * PS) % plane
                blo = jnp.where(
                    b_id == 0, pltpu.roll(glo, lo, 1) if lo else glo, pltpu.roll(value, PS, 1)
                )
                bhi = jnp.where(
                    b_id == PS - 1,
                    pltpu.roll(ghi, hi, 1) if hi else ghi,
                    pltpu.roll(value, plane - PS, 1),
                )
                return blo, bhi, pltpu.roll(value, 1, 1), pltpu.roll(value, plane - 1, 1)

            k = kap_ref[s, :, at]
            u = last_ref[s, 0, :, at]
            ka = planes(lambda t, p: kap_ref[t, :, pl.ds(p, plane)], pl.ds(rhs, 1))
            ua = planes(lambda t, p: last_ref[t, 0, :, pl.ds(p, plane)], pl.ds(0, rhs))
            kr = rolled(k, kg_lo, kg_hi)
            ur = rolled(u, ug_lo, ug_hi)
            kc = (jnp.where(c_id == 0, 0.0, kr[2]), jnp.where(c_id == PS - 1, 0.0, kr[3]))
            near_k = (ka[0], ka[1], kr[0], kr[1], kc[0], kc[1])
            near_u = (ua[0], ua[1]) + ur
            weights = [0.5 * (k + kn) for kn in near_k]
            diag = weights[0]
            for w in weights[1:]:
                diag = diag + w
            weights[4] = jnp.where(c_id == 0, 0.0, weights[4])
            weights[5] = jnp.where(c_id == PS - 1, 0.0, weights[5])
            image = diag * u
            for w, un in zip(weights, near_u):
                image = image - w * un
            image = jnp.where(live, image, 0.0)
            image_ref[s, :, at] = image
            sg = jnp.where(live, 1 - 2 * sgn_ref[s, :, at], 0).astype(f32)
            for part, value in enumerate((old_ref[s, 0, :, at], u, image)):
                head, tail = split(value * sg)
                cols[s, pl.ds(part * rhs, rhs), at] = head
                cols[s, pl.ds((part + 3) * rhs, rhs), at] = tail
        return carry

    lax.fori_loop(0, cap, one_slot, 0)

    def one_gram(s, acc):
        whole = cols[s]
        imgs = jnp.concatenate(
            [whole[2 * rhs:3 * rhs], whole[5 * rhs:6 * rhs]], axis=0
        )
        both = lax.dot_general(
            whole, imgs, (((1,), (1,)), ((), ())), preferred_element_type=f32
        )
        both = both[:2 * rhs] + both[3 * rhs:5 * rhs]
        return acc + both[:, :rhs] + both[:, rhs:]

    gram_ref[...] = lax.fori_loop(0, cap, one_gram, jnp.zeros((2 * rhs, rhs), f32))

    cell_bits = cells.bit_length() - 1
    inner = lax.broadcasted_iota(jnp.int32, (TILE, TILE), 0)
    outer = cells // TILE
    hi_ids = lax.broadcasted_iota(jnp.int32, (outer, TILE), 0)

    def one_tile(t, carry):
        at = pl.ds(pl.multiple_of(t * TILE, TILE), TILE)
        rows = rows_ref[:, at]
        inside = parity_sign(jnp.bitwise_and(inner, rows), 8).astype(f32).astype(bf16)
        across = parity_sign(
            jnp.bitwise_and(hi_ids, jnp.right_shift(rows, 8) & (outer - 1)), 4
        ).astype(f32)
        for h in range(outer):
            table[pl.ds(h * TILE, TILE), :] = inside * across[h:h + 1].astype(bf16)
        flat = cols[...].reshape(cap * 6 * rhs, cells)
        spread = jnp.dot(flat, table[...], preferred_element_type=f32)
        total = jnp.zeros((3 * rhs, TILE), f32)
        for s in range(cap):
            patch = (offset + s) * n_py + j
            w = parity_sign(
                jnp.bitwise_and(jnp.right_shift(rows, cell_bits), patch), 16
            ).astype(f32)
            base = s * 6 * rhs
            total = total + w * (
                spread[base:base + 3 * rhs] + spread[base + 3 * rhs:base + 6 * rhs]
            )
        sketch_ref[:, at] = total * scale
        return carry

    lax.fori_loop(0, rows_ref.shape[1] // TILE, one_tile, 0)


def local_work(n_py, scale, counts, last, old, kap, sgn, yg, xg, rows):
    cap, _, rhs, cells = last.shape
    k = rows.shape[1]
    return pl.pallas_call(
        functools.partial(local_kernel, n_py, scale),
        out_shape=(
            jax.ShapeDtypeStruct((cap, rhs, cells), f32),
            jax.ShapeDtypeStruct((2 * rhs, rhs), f32),
            jax.ShapeDtypeStruct((3 * rhs, k), f32),
        ),
        in_specs=[SMEM] + [VMEM] * 7,
        out_specs=(VMEM, VMEM, VMEM),
        scratch_shapes=[
            pltpu.VMEM((cap, 6 * rhs, cells), bf16),
            pltpu.VMEM((cells, TILE), bf16),
        ],
        compiler_params=params(),
    )(counts, last, old, kap, sgn, yg, xg, rows)


def block_kernel(proj_ref, old_ref, last_ref, image_ref, out_ref):
    rhs = old_ref.shape[2]
    proj = proj_ref[...]
    pair = jnp.concatenate([old_ref[0, 0], last_ref[0, 0]], axis=0)
    moved = lax.dot_general(
        proj, pair, (((0,), (0,)), ((), ())), precision=highest, preferred_element_type=f32
    )
    out_ref[0, 0] = image_ref[0] - moved


def masked_block_kernel(counts_ref, proj_ref, old_ref, last_ref, image_ref, out_ref):
    s = pl.program_id(0)
    held = counts_ref[lax.axis_index("px")]

    @pl.when(s < held)
    def _():
        block_kernel(proj_ref, old_ref, last_ref, image_ref, out_ref)

    @pl.when(s >= held)
    def _():
        out_ref[...] = jnp.zeros(out_ref.shape, f32)


def new_block_of(counts, proj, old, last, image):
    cap, _, rhs, cells = last.shape
    wide = pl.BlockSpec((1, 1, rhs, cells), lambda s: (s, 0, 0, 0))
    return pl.pallas_call(
        masked_block_kernel,
        grid=(cap,),
        out_shape=jax.ShapeDtypeStruct(last.shape, f32),
        in_specs=[
            SMEM,
            pl.BlockSpec(proj.shape, lambda s: (0, 0)),
            wide,
            wide,
            pl.BlockSpec((1, rhs, cells), lambda s: (s, 0, 0)),
        ],
        out_specs=wide,
        compiler_params=params(),
    )(counts, proj, old, last, image)


def tn(left, right):
    return lax.dot_general(
        left, right, (((0,), (0,)), ((), ())), precision=highest, preferred_element_type=f32
    )


def nt(left, right):
    return lax.dot_general(
        left, right, (((1,), (1,)), ((), ())), precision=highest, preferred_element_type=f32
    )


def normal_kernel(rhs, sk_ref, proj_ref, prev_ref, resid_ref, mine_ref, parts_ref):
    pair = sk_ref[pl.ds(0, 2 * rhs), :]
    second = sk_ref[pl.ds(2 * rhs, rhs), :]
    mine_ref[pl.ds(0, 2 * rhs), :] = pair
    mine_ref[pl.ds(2 * rhs, rhs), :] = second - tn(proj_ref[...], pair)
    images = jnp.concatenate([tn(prev_ref[...], pair), second], axis=0)
    target = tn(resid_ref[...], pair[:rhs])
    parts_ref[...] = nt(images, jnp.concatenate([images, target], axis=0))


def normal_parts(sk, proj, prev, resid):
    rhs = resid.shape[0]
    return pl.pallas_call(
        functools.partial(normal_kernel, rhs),
        out_shape=(
            jax.ShapeDtypeStruct(sk.shape, f32),
            jax.ShapeDtypeStruct((2 * rhs, 3 * rhs), f32),
        ),
        compiler_params=params(),
    )(sk, proj, prev, resid)


def eliminate(work):
    size, width = work.shape
    row_id = lax.broadcasted_iota(jnp.int32, (size, 1), 0)
    for step in range(size):
        row = work[step:step + 1, :]
        pivot = row[:, step:step + 1]
        scaled = row / pivot
        column = jnp.where(row_id == step, 0.0, work[:, step:step + 1])
        work = jnp.where(row_id == step, scaled, work - column * scaled)
    return work


def solve_kernel(parts_ref, out_ref):
    size = parts_ref.shape[0]
    out_ref[...] = eliminate(parts_ref[...])[:, size:]


def solve(parts):
    size, width = parts.shape
    return pl.pallas_call(
        solve_kernel,
        out_shape=jax.ShapeDtypeStruct((size, width - size), f32),
        compiler_params=params(),
    )(parts)


def body(
    n_px, n_py, counts, coefficient, signs, basis_old, basis_last, residual_factor, previous_coef,
    sample_rows,
):
    total_cells = MEANX * n_px * n_py * coefficient.shape[2]
    rows = sample_rows.reshape(1, -1)
    yg, xg = halo(n_px, n_py, counts, basis_last, coefficient)
    image, gram, sketch = local_work(
        n_py, 1.0 / math.sqrt(total_cells), counts, basis_last, basis_old, coefficient, signs, yg,
        xg, rows,
    )
    sketch_share = lax.psum_scatter(sketch, ("px", "py"), scatter_dimension=1, tiled=True)
    proj = lax.psum(gram, ("px", "py")) / total_cells
    mine, parts = normal_parts(sketch_share, proj, previous_coef, residual_factor)
    answer = solve(lax.psum(parts, ("px", "py")))
    new_block = new_block_of(counts, proj, basis_old, basis_last, image)
    return (new_block, mine, answer)


def solution(mesh):
    in_specs = (
        P(),
        P("px", "py", None),
        P("px", "py", None),
        P("px", "py", None, None),
        P("px", "py", None, None),
        P(),
        P(),
        P(),
    )
    out_specs = (P("px", "py", None, None), P(None, ("px", "py")), P())
    return jax.shard_map(
        functools.partial(body, mesh.shape["px"], mesh.shape["py"]),
        mesh=mesh,
        in_specs=in_specs,
        out_specs=out_specs,
        check_vma=False,
    )
```

```python
import functools
import math

import jax
import jax.numpy as jnp
from jax import lax
from jax.experimental import pallas as pl
from jax.experimental.pallas import tpu as pltpu
from jax.sharding import PartitionSpec as P

PS = 16
MEANX = 2
TILE = 256

highest = lax.Precision.HIGHEST
f32 = jnp.float32
bf16 = jnp.bfloat16
VMEM = pl.BlockSpec(memory_space=pltpu.VMEM)
SMEM = pl.BlockSpec(memory_space=pltpu.SMEM)


def params(**more):
    return pltpu.CompilerParams(vmem_limit_bytes=48 * 1024 * 1024, **more)


def parity_sign(values, bits):
    amount = 1
    while amount < bits:
        amount *= 2
    while amount > 1:
        amount //= 2
        values = jnp.bitwise_xor(values, jnp.right_shift(values, amount))
    return 1 - 2 * jnp.bitwise_and(values, 1)


def halo_kernel(
    n_px, n_py, counts_ref, last_ref, kap_ref, yg_ref, xg_ref, ybuf, xbuf, ysend, yrecv, xsend, xrecv
):
    i = lax.axis_index("px")
    j = lax.axis_index("py")
    cap = last_ref.shape[0]
    rhs = last_ref.shape[2]
    plane = PS * PS
    barrier = pltpu.get_barrier_semaphore()
    around = [
        ("py", j - 1, j > 0),
        ("py", j + 1, j < n_py - 1),
        ("px", i - 1, i > 0),
        ("px", i + 1, i < n_px - 1),
    ]
    for axis, index, valid in around:
        @pl.when(valid)
        def _(axis=axis, index=index):
            pl.semaphore_signal(
                barrier, inc=1, device_id={axis: index}, device_id_type=pl.DeviceIdType.MESH
            )

    lane = lax.broadcasted_iota(jnp.int32, (1, plane), 1)
    tail = jnp.clip(counts_ref[i] - 1, 0, cap - 1)
    xbuf[0, pl.ds(0, rhs), :] = last_ref[0, 0, :, pl.ds(0, plane)]
    xbuf[0, pl.ds(rhs, 1), :] = kap_ref[0, :, pl.ds(0, plane)]
    top = (PS - 1) * plane
    xbuf[1, pl.ds(0, rhs), :] = last_ref[tail, 0, :, pl.ds(top, plane)]
    xbuf[1, pl.ds(rhs, 1), :] = kap_ref[tail, :, pl.ds(top, plane)]

    def pack(s, carry):
        u0 = jnp.zeros((rhs, plane), f32)
        u1 = jnp.zeros((rhs, plane), f32)
        k0 = jnp.zeros((1, plane), f32)
        k1 = jnp.zeros((1, plane), f32)
        for a in range(PS):
            mine = lane // PS == a
            u = last_ref[s, 0, :, pl.ds(a * plane, plane)]
            k = kap_ref[s, :, pl.ds(a * plane, plane)]
            lo = (a * PS) % plane
            hi = (a * PS + PS) % plane
            u0 = jnp.where(mine, pltpu.roll(u, lo, 1) if lo else u, u0)
            u1 = jnp.where(mine, pltpu.roll(u, hi, 1) if hi else u, u1)
            k0 = jnp.where(mine, pltpu.roll(k, lo, 1) if lo else k, k0)
            k1 = jnp.where(mine, pltpu.roll(k, hi, 1) if hi else k, k1)
        ybuf[0, pl.ds(pl.multiple_of(s * rhs, 8), rhs), :] = u0
        ybuf[1, pl.ds(pl.multiple_of(s * rhs, 8), rhs), :] = u1
        ybuf[0, pl.ds(cap * rhs + s, 1), :] = k0
        ybuf[1, pl.ds(cap * rhs + s, 1), :] = k1
        return carry

    peers = sum(valid.astype(jnp.int32) for _, _, valid in around)
    pl.semaphore_wait(barrier, peers)

    def copy_of(base, side):
        axis, index, _ = around[base + side]
        buf, ghost, send, recv = (
            (xbuf, xg_ref, xsend, xrecv) if base == 2 else (ybuf, yg_ref, ysend, yrecv)
        )
        return pltpu.make_async_remote_copy(
            src_ref=buf.at[side],
            dst_ref=ghost.at[1 - side],
            send_sem=send.at[side],
            recv_sem=recv.at[1 - side],
            device_id={axis: index},
            device_id_type=pl.DeviceIdType.MESH,
        )

    for side in range(2):
        @pl.when(around[2 + side][2])
        def _(side=side):
            copy_of(2, side).start()

    lax.fori_loop(0, cap, pack, 0)

    for side in range(2):
        @pl.when(around[side][2])
        def _(side=side):
            copy_of(0, side).start()
    for base, ghost in ((0, yg_ref), (2, xg_ref)):
        for side in range(2):
            @pl.when(jnp.logical_not(around[base + side][2]))
            def _(ghost=ghost, side=side):
                ghost[side] = jnp.zeros(ghost.shape[1:], f32)
    for base in (2, 0):
        for side in range(2):
            @pl.when(around[base + side][2])
            def _(base=base, side=side):
                copy_of(base, side).wait_send()
    for base, ghost, buf, send, recv in (
        (2, xg_ref, xbuf, xsend, xrecv),
        (0, yg_ref, ybuf, ysend, yrecv),
    ):
        for side in range(2):
            axis, index, valid = around[base + side]

            @pl.when(valid)
            def _(ghost=ghost, buf=buf, side=side, send=send, recv=recv, axis=axis, index=index):
                pltpu.make_async_remote_copy(
                    src_ref=buf.at[side],
                    dst_ref=ghost.at[side],
                    send_sem=send.at[side],
                    recv_sem=recv.at[side],
                    device_id={axis: index},
                    device_id_type=pl.DeviceIdType.MESH,
                ).wait_recv()


def halo(n_px, n_py, counts, last, kap):
    cap, _, rhs, _ = last.shape
    plane = PS * PS
    yrows = cap * rhs + -(-cap // 8) * 8
    xrows = rhs + 8
    return pl.pallas_call(
        functools.partial(halo_kernel, n_px, n_py),
        out_shape=(
            jax.ShapeDtypeStruct((2, yrows, plane), f32),
            jax.ShapeDtypeStruct((2, xrows, plane), f32),
        ),
        in_specs=[SMEM, VMEM, VMEM],
        out_specs=(VMEM, VMEM),
        scratch_shapes=[
            pltpu.VMEM((2, yrows, plane), f32),
            pltpu.VMEM((2, xrows, plane), f32),
            pltpu.SemaphoreType.DMA((2,)),
            pltpu.SemaphoreType.DMA((2,)),
            pltpu.SemaphoreType.DMA((2,)),
            pltpu.SemaphoreType.DMA((2,)),
        ],
        compiler_params=params(collective_id=0, has_side_effects=True),
    )(counts, last, kap)


def split(values):
    head = values.astype(bf16)
    return head, (values - head.astype(f32)).astype(bf16)


def local_kernel(
    n_py, scale, counts_ref, last_ref, old_ref, kap_ref, sgn_ref, yg_ref, xg_ref, rows_ref,
    image_ref, gram_ref, sketch_ref, cols, table,
):
    i = lax.axis_index("px")
    j = lax.axis_index("py")
    cap, _, rhs, cells = last_ref.shape
    plane = PS * PS
    held = counts_ref[i]
    offset = lax.fori_loop(0, i, lambda t, acc: acc + counts_ref[t], jnp.int32(0))
    lane = lax.broadcasted_iota(jnp.int32, (1, plane), 1)
    b_id = lane // PS
    c_id = lane % PS
    top = (PS - 1) * plane

    def one_slot(s, carry):
        live = s < held
        first = s == 0
        final = s == held - 1
        before = jnp.maximum(s - 1, 0)
        after = jnp.minimum(s + 1, cap - 1)
        ks = pl.ds(cap * rhs + s, 1)
        us = pl.ds(pl.multiple_of(s * rhs, 8), rhs)
        kg_lo, kg_hi = yg_ref[0, ks, :], yg_ref[1, ks, :]
        ug_lo, ug_hi = yg_ref[0, us, :], yg_ref[1, us, :]
        for a in range(PS):
            at = pl.ds(a * plane, plane)

            def planes(ref_at, ghost_rows):
                if a == 0:
                    low = jnp.where(first, xg_ref[0, ghost_rows, :], ref_at(before, top))
                else:
                    low = ref_at(s, (a - 1) * plane)
                if a == PS - 1:
                    high = jnp.where(final, xg_ref[1, ghost_rows, :], ref_at(after, 0))
                else:
                    high = ref_at(s, (a + 1) * plane)
                return low, high

            def rolled(value, glo, ghi):
                lo = (plane - a * PS) % plane
                hi = (plane - PS - a * PS) % plane
                blo = jnp.where(
                    b_id == 0, pltpu.roll(glo, lo, 1) if lo else glo, pltpu.roll(value, PS, 1)
                )
                bhi = jnp.where(
                    b_id == PS - 1,
                    pltpu.roll(ghi, hi, 1) if hi else ghi,
                    pltpu.roll(value, plane - PS, 1),
                )
                return blo, bhi, pltpu.roll(value, 1, 1), pltpu.roll(value, plane - 1, 1)

            k = kap_ref[s, :, at]
            u = last_ref[s, 0, :, at]
            ka = planes(lambda t, p: kap_ref[t, :, pl.ds(p, plane)], pl.ds(rhs, 1))
            ua = planes(lambda t, p: last_ref[t, 0, :, pl.ds(p, plane)], pl.ds(0, rhs))
            kr = rolled(k, kg_lo, kg_hi)
            ur = rolled(u, ug_lo, ug_hi)
            kc = (jnp.where(c_id == 0, 0.0, kr[2]), jnp.where(c_id == PS - 1, 0.0, kr[3]))
            near_k = (ka[0], ka[1], kr[0], kr[1], kc[0], kc[1])
            near_u = (ua[0], ua[1]) + ur
            weights = [0.5 * (k + kn) for kn in near_k]
            diag = weights[0]
            for w in weights[1:]:
                diag = diag + w
            weights[4] = jnp.where(c_id == 0, 0.0, weights[4])
            weights[5] = jnp.where(c_id == PS - 1, 0.0, weights[5])
            image = diag * u
            for w, un in zip(weights, near_u):
                image = image - w * un
            image = jnp.where(live, image, 0.0)
            image_ref[s, :, at] = image
            sg = jnp.where(live, 1 - 2 * sgn_ref[s, :, at], 0).astype(f32)
            for part, value in enumerate((old_ref[s, 0, :, at], u, image)):
                head, tail = split(value * sg)
                cols[s, pl.ds(part * rhs, rhs), at] = head
                cols[s, pl.ds((part + 3) * rhs, rhs), at] = tail
        return carry

    lax.fori_loop(0, cap, one_slot, 0)

    def one_gram(s, acc):
        whole = cols[s]
        imgs = jnp.concatenate(
            [whole[2 * rhs:3 * rhs], whole[5 * rhs:6 * rhs]], axis=0
        )
        both = lax.dot_general(
            imgs, whole, (((1,), (1,)), ((), ())), preferred_element_type=f32
        )
        both = both[:, :2 * rhs] + both[:, 3 * rhs:5 * rhs]
        return acc + both[:rhs] + both[rhs:]

    gram_ref[...] = lax.fori_loop(0, cap, one_gram, jnp.zeros((rhs, 2 * rhs), f32))

    cell_bits = cells.bit_length() - 1
    width = sketch_ref.shape[2]
    inner = lax.broadcasted_iota(jnp.int32, (TILE, TILE), 0)
    outer = cells // TILE
    hi_ids = lax.broadcasted_iota(jnp.int32, (outer, TILE), 0)

    def one_tile(t, carry):
        at = pl.ds(pl.multiple_of(t * TILE, TILE), TILE)
        rows = rows_ref[:, at]
        inside = parity_sign(jnp.bitwise_and(inner, rows), 8).astype(f32).astype(bf16)
        across = parity_sign(
            jnp.bitwise_and(hi_ids, jnp.right_shift(rows, 8) & (outer - 1)), 4
        ).astype(f32)
        for h in range(outer):
            table[pl.ds(h * TILE, TILE), :] = inside * across[h:h + 1].astype(bf16)
        flat = cols[...].reshape(cap * 6 * rhs, cells)
        spread = jnp.dot(flat, table[...], preferred_element_type=f32)
        total = jnp.zeros((3 * rhs, TILE), f32)
        for s in range(cap):
            patch = (offset + s) * n_py + j
            w = parity_sign(
                jnp.bitwise_and(jnp.right_shift(rows, cell_bits), patch), 16
            ).astype(f32)
            base = s * 6 * rhs
            total = total + w * (
                spread[base:base + 3 * rhs] + spread[base + 3 * rhs:base + 6 * rhs]
            )
        total = total * scale
        for r in range(TILE // width):
            sketch_ref[t * (TILE // width) + r] = total[:, r * width:(r + 1) * width]
        return carry

    lax.fori_loop(0, rows_ref.shape[1] // TILE, one_tile, 0)


def local_work(n_px, n_py, scale, counts, last, old, kap, sgn, yg, xg, rows):
    cap, _, rhs, cells = last.shape
    k = rows.shape[1]
    return pl.pallas_call(
        functools.partial(local_kernel, n_py, scale),
        out_shape=(
            jax.ShapeDtypeStruct((cap, rhs, cells), f32),
            jax.ShapeDtypeStruct((rhs, 2 * rhs), f32),
            jax.ShapeDtypeStruct((n_px, 3 * rhs, k // n_px), f32),
        ),
        in_specs=[SMEM] + [VMEM] * 7,
        out_specs=(VMEM, VMEM, VMEM),
        scratch_shapes=[
            pltpu.VMEM((cap, 6 * rhs, cells), bf16),
            pltpu.VMEM((cells, TILE), bf16),
        ],
        compiler_params=params(),
    )(counts, last, old, kap, sgn, yg, xg, rows)


def block_kernel(proj_ref, old_ref, last_ref, image_ref, out_ref):
    rhs = old_ref.shape[2]
    proj = proj_ref[...]
    pair = jnp.concatenate([old_ref[0, 0], last_ref[0, 0]], axis=0)
    moved = lax.dot_general(
        proj, pair, (((1,), (0,)), ((), ())), precision=highest, preferred_element_type=f32
    )
    out_ref[0, 0] = image_ref[0] - moved


def masked_block_kernel(counts_ref, proj_ref, old_ref, last_ref, image_ref, out_ref):
    s = pl.program_id(0)
    held = counts_ref[lax.axis_index("px")]

    @pl.when(s < held)
    def _():
        block_kernel(proj_ref, old_ref, last_ref, image_ref, out_ref)

    @pl.when(s >= held)
    def _():
        out_ref[...] = jnp.zeros(out_ref.shape, f32)


def new_block_of(counts, proj, old, last, image):
    cap, _, rhs, cells = last.shape
    wide = pl.BlockSpec((1, 1, rhs, cells), lambda s: (s, 0, 0, 0))
    return pl.pallas_call(
        masked_block_kernel,
        grid=(cap,),
        out_shape=jax.ShapeDtypeStruct(last.shape, f32),
        in_specs=[
            SMEM,
            pl.BlockSpec(proj.shape, lambda s: (0, 0)),
            wide,
            wide,
            pl.BlockSpec((1, rhs, cells), lambda s: (s, 0, 0)),
        ],
        out_specs=wide,
        compiler_params=params(),
    )(counts, proj, old, last, image)


def tn(left, right):
    return lax.dot_general(
        left, right, (((0,), (0,)), ((), ())), precision=highest, preferred_element_type=f32
    )


def nt(left, right):
    return lax.dot_general(
        left, right, (((1,), (1,)), ((), ())), precision=highest, preferred_element_type=f32
    )


def eliminate(work):
    size, width = work.shape
    row_id = lax.broadcasted_iota(jnp.int32, (size, 1), 0)
    for step in range(size):
        row = work[step:step + 1, :]
        pivot = row[:, step:step + 1]
        scaled = row / pivot
        column = jnp.where(row_id == step, 0.0, work[:, step:step + 1])
        work = jnp.where(row_id == step, scaled, work - column * scaled)
    return work


def nn(left, right):
    return jnp.dot(left, right, precision=highest, preferred_element_type=f32)


def reduce_kernel(
    n_px, n_py, total_cells, gram_ref, sketch_ref, prev_ref, resid_ref, proj_ref, mine_ref,
    answer_ref, gram_x, sketch_x, gram_y, sketch_y, parts_x, gram_xs, gram_xr, sketch_xs,
    sketch_xr, gram_ys, gram_yr, sketch_ys, sketch_yr, parts_s, parts_r,
):
    i = lax.axis_index("px")
    j = lax.axis_index("py")
    rhs = resid_ref.shape[0]
    x_peers = [lax.rem(i + d, n_px) for d in range(1, n_px)]
    y_peers = [lax.rem(j + d, n_py) for d in range(1, n_py)]
    barrier = pltpu.get_barrier_semaphore()
    for axis, peers in (("px", x_peers), ("py", y_peers)):
        for peer in peers:
            pl.semaphore_signal(
                barrier, inc=1, device_id={axis: peer}, device_id_type=pl.DeviceIdType.MESH
            )
    pl.semaphore_wait(barrier, n_px + n_py - 2)

    def exchange(axis, me, peers, source, slots, send, recv):
        def copy(peer, slot):
            return pltpu.make_async_remote_copy(
                src_ref=source(peer),
                dst_ref=slots.at[slot],
                send_sem=send.at[peer],
                recv_sem=recv.at[slot],
                device_id={axis: peer},
                device_id_type=pl.DeviceIdType.MESH,
            )

        for peer in peers:
            copy(peer, me).start()

        def finish():
            for peer in peers:
                copy(peer, peer).wait_recv()
            for peer in peers:
                copy(peer, me).wait_send()

        return finish

    def total(slots):
        acc = slots[0]
        for p in range(1, slots.shape[0]):
            acc = acc + slots[p]
        return acc

    gram_done = exchange("px", i, x_peers, lambda p: gram_ref, gram_x, gram_xs, gram_xr)
    sketch_done = exchange(
        "px", i, x_peers, lambda p: sketch_ref.at[p], sketch_x, sketch_xs, sketch_xr
    )
    gram_x[i] = gram_ref[...]
    sketch_x[i] = sketch_ref[i]
    gram_done()
    gram_y[j] = total(gram_x)
    gram_done = exchange("py", j, y_peers, lambda p: gram_y.at[j], gram_y, gram_ys, gram_yr)
    sketch_done()
    sketch_y[j] = total(sketch_x)
    sketch_done = exchange("py", j, y_peers, lambda p: sketch_y.at[j], sketch_y, sketch_ys, sketch_yr)
    gram_done()
    proj = total(gram_y) * (1.0 / total_cells)
    proj_ref[...] = proj
    sketch_done()
    whole = total(sketch_y)
    pair = whole[:2 * rhs]
    second = whole[2 * rhs:]
    images = jnp.concatenate([tn(prev_ref[...], pair), second], axis=0)
    target = tn(resid_ref[...], pair[:rhs])
    parts_x[i] = nt(images, jnp.concatenate([images, target], axis=0))
    parts_done = exchange("px", i, x_peers, lambda p: parts_x.at[i], parts_x, parts_s, parts_r)
    newer = second - nn(proj, pair)
    width, share = whole.shape[1], mine_ref.shape[1]
    chosen = (
        lax.broadcasted_iota(jnp.int32, (width, share), 0)
        == lax.broadcasted_iota(jnp.int32, (width, share), 1) + j * share
    ).astype(f32)
    mine_ref[...] = nn(jnp.concatenate([pair, newer], axis=0), chosen)
    parts_done()
    answer_ref[...] = eliminate(total(parts_x))[:, 2 * rhs:]


def reduce_work(n_px, n_py, total_cells, gram, sketch, prev, resid):
    rhs = resid.shape[0]
    width = sketch.shape[2]
    sems = lambda n: pltpu.SemaphoreType.DMA((n,))
    return pl.pallas_call(
        functools.partial(reduce_kernel, n_px, n_py, total_cells),
        out_shape=(
            jax.ShapeDtypeStruct(gram.shape, f32),
            jax.ShapeDtypeStruct((3 * rhs, width // n_py), f32),
            jax.ShapeDtypeStruct((2 * rhs, rhs), f32),
        ),
        in_specs=[VMEM] * 4,
        out_specs=(VMEM, VMEM, VMEM),
        scratch_shapes=[
            pltpu.VMEM((n_px,) + gram.shape, f32),
            pltpu.VMEM(sketch.shape, f32),
            pltpu.VMEM((n_py,) + gram.shape, f32),
            pltpu.VMEM((n_py,) + sketch.shape[1:], f32),
            pltpu.VMEM((n_px, 2 * rhs, 3 * rhs), f32),
            sems(n_px), sems(n_px), sems(n_px), sems(n_px),
            sems(n_py), sems(n_py), sems(n_py), sems(n_py),
            sems(n_px), sems(n_px),
        ],
        compiler_params=params(collective_id=1, has_side_effects=True),
    )(gram, sketch, prev, resid)


def body(
    n_px, n_py, counts, coefficient, signs, basis_old, basis_last, residual_factor, previous_coef,
    sample_rows,
):
    total_cells = MEANX * n_px * n_py * coefficient.shape[2]
    rows = sample_rows.reshape(1, -1)
    yg, xg = halo(n_px, n_py, counts, basis_last, coefficient)
    image, gram, sketch = local_work(
        n_px, n_py, 1.0 / math.sqrt(total_cells), counts, basis_last, basis_old, coefficient, signs,
        yg, xg, rows,
    )
    proj, mine, answer = reduce_work(
        n_px, n_py, total_cells, gram, sketch, previous_coef, residual_factor
    )
    new_block = new_block_of(counts, proj, basis_old, basis_last, image)
    return (new_block, mine, answer)


def solution(mesh):
    in_specs = (
        P(),
        P("px", "py", None),
        P("px", "py", None),
        P("px", "py", None, None),
        P("px", "py", None, None),
        P(),
        P(),
        P(),
    )
    out_specs = (P("px", "py", None, None), P(None, ("px", "py")), P())
    return jax.shard_map(
        functools.partial(body, mesh.shape["px"], mesh.shape["py"]),
        mesh=mesh,
        in_specs=in_specs,
        out_specs=out_specs,
        check_vma=False,
    )
```

```python
import functools
import math

import jax
import jax.numpy as jnp
from jax import lax
from jax.experimental import pallas as pl
from jax.experimental.pallas import tpu as pltpu
from jax.sharding import PartitionSpec as P

PS = 16
MEANX = 2
TILE = 256

highest = lax.Precision.HIGHEST
f32 = jnp.float32
bf16 = jnp.bfloat16
VMEM = pl.BlockSpec(memory_space=pltpu.VMEM)
SMEM = pl.BlockSpec(memory_space=pltpu.SMEM)


def params(**more):
    return pltpu.CompilerParams(vmem_limit_bytes=48 * 1024 * 1024, **more)


def parity_sign(values, bits):
    amount = 1
    while amount < bits:
        amount *= 2
    while amount > 1:
        amount //= 2
        values = jnp.bitwise_xor(values, jnp.right_shift(values, amount))
    return 1 - 2 * jnp.bitwise_and(values, 1)


def split(values):
    head = values.astype(bf16)
    return head, (values - head.astype(f32)).astype(bf16)


def tn(left, right):
    return lax.dot_general(
        left, right, (((0,), (0,)), ((), ())), precision=highest, preferred_element_type=f32
    )


def nt(left, right):
    return lax.dot_general(
        left, right, (((1,), (1,)), ((), ())), precision=highest, preferred_element_type=f32
    )


def eliminate(work):
    size, width = work.shape
    row_id = lax.broadcasted_iota(jnp.int32, (size, 1), 0)
    for step in range(size):
        row = work[step:step + 1, :]
        pivot = row[:, step:step + 1]
        scaled = row / pivot
        column = jnp.where(row_id == step, 0.0, work[:, step:step + 1])
        work = jnp.where(row_id == step, scaled, work - column * scaled)
    return work


def nn(left, right):
    return jnp.dot(left, right, precision=highest, preferred_element_type=f32)


def step_kernel(
    n_px, n_py, total_cells, counts_ref, last_hbm, old_hbm, kap_hbm, sgn_hbm, rows_ref, prev_ref,
    resid_ref, new_hbm, mine_ref, answer_ref, last_ref, old_ref, kap_ref, sgn_ref, in_sem, out_sem,
    xbuf, ybuf, xg_ref, yg_ref, xsend, xrecv, ysend, yrecv, image_ref, cols, table, gram_ref,
    sketch_ref, gram_x, sketch_x, gram_y, sketch_y, parts_x, gram_xs, gram_xr, sketch_xs,
    sketch_xr, gram_ys, gram_yr, sketch_ys, sketch_yr, parts_s, parts_r,
):
    i = lax.axis_index("px")
    j = lax.axis_index("py")
    cap, _, rhs, cells = last_ref.shape
    plane = PS * PS
    top = (PS - 1) * plane
    mesh_id = pl.DeviceIdType.MESH
    loads = [
        pltpu.make_async_copy(source, target, in_sem.at[index])
        for index, (source, target) in enumerate(
            ((last_hbm, last_ref), (kap_hbm, kap_ref), (old_hbm, old_ref), (sgn_hbm, sgn_ref))
        )
    ]
    for load in loads:
        load.start()
    x_peers = [lax.rem(i + d, n_px) for d in range(1, n_px)]
    y_peers = [lax.rem(j + d, n_py) for d in range(1, n_py)]
    barrier = pltpu.get_barrier_semaphore()
    for axis, peers in (("px", x_peers), ("py", y_peers)):
        for peer in peers:
            pl.semaphore_signal(barrier, inc=1, device_id={axis: peer}, device_id_type=mesh_id)
    around = [
        ("py", j - 1, j > 0),
        ("py", j + 1, j < n_py - 1),
        ("px", i - 1, i > 0),
        ("px", i + 1, i < n_px - 1),
    ]
    lane = lax.broadcasted_iota(jnp.int32, (1, plane), 1)
    b_id = lane // PS
    c_id = lane % PS
    held = counts_ref[i]
    offset = jnp.int32(0)
    for t in range(n_px):
        offset = offset + jnp.where(t < i, counts_ref[t], 0)
    tail = jnp.clip(held - 1, 0, cap - 1)

    loads[0].wait()
    loads[1].wait()
    xbuf[0, pl.ds(0, rhs), :] = last_ref[0, 0, :, pl.ds(0, plane)]
    xbuf[0, pl.ds(rhs, 1), :] = kap_ref[0, :, pl.ds(0, plane)]
    xbuf[1, pl.ds(0, rhs), :] = last_ref[tail, 0, :, pl.ds(top, plane)]
    xbuf[1, pl.ds(rhs, 1), :] = kap_ref[tail, :, pl.ds(top, plane)]

    def pack(s, carry):
        u0 = jnp.zeros((rhs, plane), f32)
        u1 = jnp.zeros((rhs, plane), f32)
        k0 = jnp.zeros((1, plane), f32)
        k1 = jnp.zeros((1, plane), f32)
        for a in range(PS):
            mine = b_id == a
            u = last_ref[s, 0, :, pl.ds(a * plane, plane)]
            k = kap_ref[s, :, pl.ds(a * plane, plane)]
            lo = (a * PS) % plane
            hi = (a * PS + PS) % plane
            u0 = jnp.where(mine, pltpu.roll(u, lo, 1) if lo else u, u0)
            u1 = jnp.where(mine, pltpu.roll(u, hi, 1) if hi else u, u1)
            k0 = jnp.where(mine, pltpu.roll(k, lo, 1) if lo else k, k0)
            k1 = jnp.where(mine, pltpu.roll(k, hi, 1) if hi else k, k1)
        ybuf[0, pl.ds(pl.multiple_of(s * rhs, 8), rhs), :] = u0
        ybuf[1, pl.ds(pl.multiple_of(s * rhs, 8), rhs), :] = u1
        ybuf[0, pl.ds(cap * rhs + s, 1), :] = k0
        ybuf[1, pl.ds(cap * rhs + s, 1), :] = k1
        return carry

    faces = {0: (ybuf, yg_ref, ysend, yrecv), 2: (xbuf, xg_ref, xsend, xrecv)}

    def face_copy(base, side, ghost_side):
        axis, index, _ = around[base + side]
        buf, ghost, send, recv = faces[base]
        return pltpu.make_async_remote_copy(
            src_ref=buf.at[side],
            dst_ref=ghost.at[ghost_side],
            send_sem=send.at[side],
            recv_sem=recv.at[ghost_side],
            device_id={axis: index},
            device_id_type=mesh_id,
        )

    def when_near(base, side, action):
        @pl.when(around[base + side][2])
        def _():
            action()

    pl.semaphore_wait(barrier, n_px + n_py - 2)
    for side in range(2):
        when_near(2, side, lambda: face_copy(2, side, 1 - side).start())
    lax.fori_loop(0, cap, pack, 0)
    for side in range(2):
        when_near(0, side, lambda: face_copy(0, side, 1 - side).start())
    for base in (0, 2):
        for side in range(2):
            @pl.when(jnp.logical_not(around[base + side][2]))
            def _():
                ghost = faces[base][1]
                ghost[side] = jnp.zeros(ghost.shape[1:], f32)

    loads[2].wait()
    loads[3].wait()

    def flips(s, at):
        return jnp.where(s < held, 1 - 2 * sgn_ref[s, :, at], 0).astype(f32)

    def keep(s, part, at, value):
        first_part, rest = split(value)
        cols[s, pl.ds(part * rhs, rhs), at] = first_part
        cols[s, pl.ds((part + 3) * rhs, rhs), at] = rest

    def pair_columns(s, carry):
        for a in range(PS):
            at = pl.ds(a * plane, plane)
            sg = flips(s, at)
            keep(s, 0, at, old_ref[s, 0, :, at] * sg)
            keep(s, 1, at, last_ref[s, 0, :, at] * sg)
        return carry

    lax.fori_loop(0, cap, pair_columns, 0)

    for base in (2, 0):
        for side in range(2):
            when_near(base, side, lambda: face_copy(base, side, 1 - side).wait_send())
            when_near(base, side, lambda: face_copy(base, side, side).wait_recv())

    def operate(s, carry):
        live = s < held
        first = s == 0
        final = s == held - 1
        before = jnp.maximum(s - 1, 0)
        after = jnp.minimum(s + 1, cap - 1)
        ks = pl.ds(cap * rhs + s, 1)
        us = pl.ds(pl.multiple_of(s * rhs, 8), rhs)
        kg_lo, kg_hi = yg_ref[0, ks, :], yg_ref[1, ks, :]
        ug_lo, ug_hi = yg_ref[0, us, :], yg_ref[1, us, :]
        for a in range(PS):
            at = pl.ds(a * plane, plane)

            def planes(ref_at, ghost_rows):
                if a == 0:
                    low = jnp.where(first, xg_ref[0, ghost_rows, :], ref_at(before, top))
                else:
                    low = ref_at(s, (a - 1) * plane)
                if a == PS - 1:
                    high = jnp.where(final, xg_ref[1, ghost_rows, :], ref_at(after, 0))
                else:
                    high = ref_at(s, (a + 1) * plane)
                return low, high

            def rolled(value, glo, ghi):
                lo = (plane - a * PS) % plane
                hi = (plane - PS - a * PS) % plane
                blo = jnp.where(
                    b_id == 0, pltpu.roll(glo, lo, 1) if lo else glo, pltpu.roll(value, PS, 1)
                )
                bhi = jnp.where(
                    b_id == PS - 1,
                    pltpu.roll(ghi, hi, 1) if hi else ghi,
                    pltpu.roll(value, plane - PS, 1),
                )
                return blo, bhi, pltpu.roll(value, 1, 1), pltpu.roll(value, plane - 1, 1)

            k = kap_ref[s, :, at]
            u = last_ref[s, 0, :, at]
            ka = planes(lambda t, p: kap_ref[t, :, pl.ds(p, plane)], pl.ds(rhs, 1))
            ua = planes(lambda t, p: last_ref[t, 0, :, pl.ds(p, plane)], pl.ds(0, rhs))
            kr = rolled(k, kg_lo, kg_hi)
            ur = rolled(u, ug_lo, ug_hi)
            kc = (jnp.where(c_id == 0, 0.0, kr[2]), jnp.where(c_id == PS - 1, 0.0, kr[3]))
            near_k = (ka[0], ka[1], kr[0], kr[1], kc[0], kc[1])
            near_u = (ua[0], ua[1]) + ur
            weights = [0.5 * (k + kn) for kn in near_k]
            diag = weights[0]
            for w in weights[1:]:
                diag = diag + w
            weights[4] = jnp.where(c_id == 0, 0.0, weights[4])
            weights[5] = jnp.where(c_id == PS - 1, 0.0, weights[5])
            image = diag * u
            for w, un in zip(weights, near_u):
                image = image - w * un
            image = jnp.where(live, image, 0.0)
            image_ref[s, 0, :, at] = image
            keep(s, 2, at, image * flips(s, at))
        return carry

    lax.fori_loop(0, cap, operate, 0)

    def one_gram(s, acc):
        whole = cols[s]
        imgs = jnp.concatenate([whole[2 * rhs:3 * rhs], whole[5 * rhs:6 * rhs]], axis=0)
        both = lax.dot_general(
            imgs, whole, (((1,), (1,)), ((), ())), preferred_element_type=f32
        )
        both = both[:, :2 * rhs] + both[:, 3 * rhs:5 * rhs]
        return acc + both[:rhs] + both[rhs:]

    gram_ref[...] = lax.fori_loop(0, cap, one_gram, jnp.zeros((rhs, 2 * rhs), f32))

    def mover(axis, source, slots, send, recv):
        def copy(peer, slot):
            return pltpu.make_async_remote_copy(
                src_ref=source(peer),
                dst_ref=slots.at[slot],
                send_sem=send.at[peer],
                recv_sem=recv.at[slot],
                device_id={axis: peer},
                device_id_type=mesh_id,
            )

        return copy

    def start(copy, me, peers):
        for peer in peers:
            copy(peer, me).start()

    def finish(copy, me, peers):
        for peer in peers:
            copy(peer, peer).wait_recv()
        for peer in peers:
            copy(peer, me).wait_send()

    def total(slots):
        acc = slots[0]
        for p in range(1, slots.shape[0]):
            acc = acc + slots[p]
        return acc

    gram_x_copy = mover("px", lambda p: gram_ref, gram_x, gram_xs, gram_xr)
    gram_y_copy = mover("py", lambda p: gram_y.at[j], gram_y, gram_ys, gram_yr)
    sketch_x_copy = mover("px", lambda p: sketch_ref.at[p], sketch_x, sketch_xs, sketch_xr)
    sketch_y_copy = mover("py", lambda p: sketch_y.at[j], sketch_y, sketch_ys, sketch_yr)
    parts_copy = mover("px", lambda p: parts_x.at[i], parts_x, parts_s, parts_r)

    start(gram_x_copy, i, x_peers)
    gram_x[i] = gram_ref[...]

    cell_bits = cells.bit_length() - 1
    width = sketch_ref.shape[2]
    per = TILE // width
    inner = lax.broadcasted_iota(jnp.int32, (TILE, TILE), 0)
    outer = cells // TILE
    hi_ids = lax.broadcasted_iota(jnp.int32, (outer, TILE), 0)
    tiles = rows_ref.shape[1] // TILE
    scale = 1.0 / math.sqrt(total_cells)

    def one_tile(turn, carry):
        t = lax.rem(i // per + 1 + turn, tiles)
        at = pl.ds(pl.multiple_of(t * TILE, TILE), TILE)
        rows = rows_ref[:, at]
        inside = parity_sign(jnp.bitwise_and(inner, rows), 8).astype(f32).astype(bf16)
        across = parity_sign(
            jnp.bitwise_and(hi_ids, jnp.right_shift(rows, 8) & (outer - 1)), 4
        ).astype(f32)
        for h in range(outer):
            table[pl.ds(h * TILE, TILE), :] = inside * across[h:h + 1].astype(bf16)
        flat = cols[...].reshape(cap * 6 * rhs, cells)
        spread = jnp.dot(flat, table[...], preferred_element_type=f32)
        summed = jnp.zeros((3 * rhs, TILE), f32)
        for s in range(cap):
            patch = (offset + s) * n_py + j
            w = parity_sign(
                jnp.bitwise_and(jnp.right_shift(rows, cell_bits), patch), 16
            ).astype(f32)
            base = s * 6 * rhs
            summed = summed + w * (
                spread[base:base + 3 * rhs] + spread[base + 3 * rhs:base + 6 * rhs]
            )
        summed = summed * scale
        for r in range(per):
            owner = t * per + r
            sketch_ref[owner] = summed[:, r * width:(r + 1) * width]

            @pl.when(owner != i)
            def _():
                sketch_x_copy(owner, i).start()
        return carry

    half = tiles // 2
    lax.fori_loop(0, half, one_tile, 0)
    finish(gram_x_copy, i, x_peers)
    gram_y[j] = total(gram_x)
    start(gram_y_copy, j, y_peers)
    lax.fori_loop(half, tiles, one_tile, 0)
    sketch_x[i] = sketch_ref[i]
    finish(gram_y_copy, j, y_peers)
    proj = total(gram_y) * (1.0 / total_cells)
    finish(sketch_x_copy, i, x_peers)
    sketch_y[j] = total(sketch_x)
    start(sketch_y_copy, j, y_peers)

    proj_head, proj_rest = split(proj)
    none = jnp.zeros((rhs, rhs), bf16)
    both_proj = jnp.concatenate(
        [
            jnp.concatenate([proj_head, none, proj_head, none], axis=1),
            jnp.concatenate([proj_rest, none, jnp.zeros((rhs, 3 * rhs), bf16)], axis=1),
        ],
        axis=0,
    )

    def store_of(s):
        return pltpu.make_async_copy(image_ref.at[s], new_hbm.at[s], out_sem.at[s])

    def one_block(s, carry):
        moved = jnp.dot(both_proj, cols[s], preferred_element_type=f32)
        moved = moved[:rhs] + moved[rhs:]
        image_ref[s, 0] = image_ref[s, 0] - moved * flips(s, pl.ds(0, cells))
        store_of(s).start()
        return carry

    lax.fori_loop(0, cap // 2, one_block, 0)
    finish(sketch_y_copy, j, y_peers)
    whole = total(sketch_y)
    pair = whole[:2 * rhs]
    second = whole[2 * rhs:]
    images = jnp.concatenate([tn(prev_ref[...], pair), second], axis=0)
    target = tn(resid_ref[...], pair[:rhs])
    parts_x[i] = nt(images, jnp.concatenate([images, target], axis=0))
    start(parts_copy, i, x_peers)
    lax.fori_loop(cap // 2, cap, one_block, 0)
    newer = second - nn(proj, pair)
    share = mine_ref.shape[1]
    chosen = (
        lax.broadcasted_iota(jnp.int32, (width, share), 0)
        == lax.broadcasted_iota(jnp.int32, (width, share), 1) + j * share
    ).astype(f32)
    mine_ref[...] = nn(jnp.concatenate([pair, newer], axis=0), chosen)
    finish(parts_copy, i, x_peers)
    answer_ref[...] = eliminate(total(parts_x))[:, 2 * rhs:]
    for s in range(cap):
        store_of(s).wait()


def step(n_px, n_py, total_cells, counts, last, old, kap, sgn, rows, prev, resid):
    cap, _, rhs, cells = last.shape
    width = rows.shape[1] // n_px
    plane = PS * PS
    yrows = cap * rhs + -(-cap // 8) * 8
    xrows = rhs + 8
    hbm = pl.BlockSpec(memory_space=pl.ANY)
    sems = lambda n: pltpu.SemaphoreType.DMA((n,))
    return pl.pallas_call(
        functools.partial(step_kernel, n_px, n_py, total_cells),
        out_shape=(
            jax.ShapeDtypeStruct(last.shape, f32),
            jax.ShapeDtypeStruct((3 * rhs, width // n_py), f32),
            jax.ShapeDtypeStruct((2 * rhs, rhs), f32),
        ),
        in_specs=[SMEM] + [hbm] * 4 + [VMEM] * 3,
        out_specs=(hbm, VMEM, VMEM),
        scratch_shapes=[
            pltpu.VMEM(last.shape, f32),
            pltpu.VMEM(old.shape, f32),
            pltpu.VMEM(kap.shape, f32),
            pltpu.VMEM(sgn.shape, jnp.int32),
            sems(4), sems(cap),
            pltpu.VMEM((2, xrows, plane), f32),
            pltpu.VMEM((2, yrows, plane), f32),
            pltpu.VMEM((2, xrows, plane), f32),
            pltpu.VMEM((2, yrows, plane), f32),
            sems(2), sems(2), sems(2), sems(2),
            pltpu.VMEM(last.shape, f32),
            pltpu.VMEM((cap, 6 * rhs, cells), bf16),
            pltpu.VMEM((cells, TILE), bf16),
            pltpu.VMEM((rhs, 2 * rhs), f32),
            pltpu.VMEM((n_px, 3 * rhs, width), f32),
            pltpu.VMEM((n_px, rhs, 2 * rhs), f32),
            pltpu.VMEM((n_px, 3 * rhs, width), f32),
            pltpu.VMEM((n_py, rhs, 2 * rhs), f32),
            pltpu.VMEM((n_py, 3 * rhs, width), f32),
            pltpu.VMEM((n_px, 2 * rhs, 3 * rhs), f32),
            sems(n_px), sems(n_px), sems(n_px), sems(n_px),
            sems(n_py), sems(n_py), sems(n_py), sems(n_py),
            sems(n_px), sems(n_px),
        ],
        compiler_params=params(collective_id=0, has_side_effects=True),
    )(counts, last, old, kap, sgn, rows, prev, resid)


def body(
    n_px, n_py, counts, coefficient, signs, basis_old, basis_last, residual_factor, previous_coef,
    sample_rows,
):
    total_cells = MEANX * n_px * n_py * coefficient.shape[2]
    rows = sample_rows.reshape(1, -1)
    return step(
        n_px, n_py, total_cells, counts, basis_last, basis_old, coefficient, signs, rows,
        previous_coef, residual_factor,
    )


def solution(mesh):
    in_specs = (
        P(),
        P("px", "py", None),
        P("px", "py", None),
        P("px", "py", None, None),
        P("px", "py", None, None),
        P(),
        P(),
        P(),
    )
    out_specs = (P("px", "py", None, None), P(None, ("px", "py")), P())
    return jax.shard_map(
        functools.partial(body, mesh.shape["px"], mesh.shape["py"]),
        mesh=mesh,
        in_specs=in_specs,
        out_specs=out_specs,
        check_vma=False,
    )
```

```python
import functools
import math

import jax
import jax.numpy as jnp
from jax import lax
from jax.experimental import pallas as pl
from jax.experimental.pallas import tpu as pltpu
from jax.sharding import PartitionSpec as P

PS = 16
MEANX = 2
TILE = 256

highest = lax.Precision.HIGHEST
f32 = jnp.float32
bf16 = jnp.bfloat16
VMEM = pl.BlockSpec(memory_space=pltpu.VMEM)
SMEM = pl.BlockSpec(memory_space=pltpu.SMEM)


def params(**more):
    return pltpu.CompilerParams(vmem_limit_bytes=63 * 1024 * 1024, **more)


def parity_sign(values, bits):
    amount = 1
    while amount < bits:
        amount *= 2
    while amount > 1:
        amount //= 2
        values = jnp.bitwise_xor(values, jnp.right_shift(values, amount))
    return 1 - 2 * jnp.bitwise_and(values, 1)


def split(values):
    head = values.astype(bf16)
    return head, (values - head.astype(f32)).astype(bf16)


def tn(left, right):
    return lax.dot_general(
        left, right, (((0,), (0,)), ((), ())), precision=highest, preferred_element_type=f32
    )


def nt(left, right):
    return lax.dot_general(
        left, right, (((1,), (1,)), ((), ())), precision=highest, preferred_element_type=f32
    )


def eliminate(work):
    size, width = work.shape
    row_id = lax.broadcasted_iota(jnp.int32, (size, 1), 0)
    for step in range(size):
        row = work[step:step + 1, :]
        pivot = row[:, step:step + 1]
        scaled = row / pivot
        column = jnp.where(row_id == step, 0.0, work[:, step:step + 1])
        work = jnp.where(row_id == step, scaled, work - column * scaled)
    return work


def nn(left, right):
    return jnp.dot(left, right, precision=highest, preferred_element_type=f32)


def step_kernel(
    n_px, n_py, total_cells, counts_ref, last_hbm, old_hbm, kap_hbm, sgn_hbm, rows_ref, prev_ref,
    resid_ref, new_hbm, mine_ref, answer_ref, last_ref, old_ref, kap_ref, sgn_ref, in_sem, out_sem,
    xbuf, ybuf, xg_ref, yg_ref, xsend, xrecv, ysend, yrecv, image_ref, cols, table, gram_ref,
    sketch_ref, gram_x, sketch_x, gram_y, sketch_y, parts_x, gram_xs, gram_xr, sketch_xs,
    sketch_xr, gram_ys, gram_yr, sketch_ys, sketch_yr, parts_s, parts_r, table_odd, weights_ref,
    flips_ref, core_own, core_out, core_in, core_s, core_r,
):
    i = lax.axis_index("px")
    j = lax.axis_index("py")
    cap, _, rhs, cells = last_ref.shape
    plane = PS * PS
    top = (PS - 1) * plane
    mesh_id = pl.DeviceIdType.MESH
    kap_ref[...] = jnp.zeros(kap_ref.shape, f32)
    sgn_ref[...] = jnp.zeros(sgn_ref.shape, jnp.int32)
    pairs = [(last_hbm, last_ref)]
    pairs += [(kap_hbm.at[s], kap_ref.at[pl.ds(s, 1)]) for s in range(cap)]
    pairs += [(old_hbm, old_ref)]
    pairs += [(sgn_hbm.at[s], sgn_ref.at[pl.ds(s, 1)]) for s in range(cap)]
    loads = [
        pltpu.make_async_copy(source, target, in_sem.at[index])
        for index, (source, target) in enumerate(pairs)
    ]
    for load in loads:
        load.start()
    x_peers = [lax.rem(i + d, n_px) for d in range(1, n_px)]
    y_peers = [lax.rem(j + d, n_py) for d in range(1, n_py)]
    barrier = pltpu.get_barrier_semaphore()
    for axis, peers in (("px", x_peers), ("py", y_peers)):
        for peer in peers:
            pl.semaphore_signal(barrier, inc=1, device_id={axis: peer}, device_id_type=mesh_id)
    around = [
        ("py", j - 1, j > 0),
        ("py", j + 1, j < n_py - 1),
        ("px", i - 1, i > 0),
        ("px", i + 1, i < n_px - 1),
    ]
    lane = lax.broadcasted_iota(jnp.int32, (1, plane), 1)
    b_id = lane // PS
    c_id = lane % PS
    held = counts_ref[i]
    offset = jnp.int32(0)
    for t in range(n_px):
        offset = offset + jnp.where(t < i, counts_ref[t], 0)
    tail = jnp.clip(held - 1, 0, cap - 1)

    for load in loads[:cap + 1]:
        load.wait()
    xbuf[0, pl.ds(0, rhs), :] = last_ref[0, 0, :, pl.ds(0, plane)]
    xbuf[0, pl.ds(rhs, 1), :] = kap_ref[pl.ds(0, 1), pl.ds(0, plane)]
    xbuf[1, pl.ds(0, rhs), :] = last_ref[tail, 0, :, pl.ds(top, plane)]
    xbuf[1, pl.ds(rhs, 1), :] = kap_ref[pl.ds(tail, 1), pl.ds(top, plane)]

    def gather_faces(plane_at, shape):
        low = jnp.zeros(shape, f32)
        high = jnp.zeros(shape, f32)
        for a in range(PS):
            value = plane_at(pl.ds(a * plane, plane))
            lo = (a * PS) % plane
            hi = (a * PS + PS) % plane
            low = jnp.where(b_id == a, pltpu.roll(value, lo, 1) if lo else value, low)
            high = jnp.where(b_id == a, pltpu.roll(value, hi, 1) if hi else value, high)
        return low, high

    def pack(s, carry):
        low, high = gather_faces(lambda at: last_ref[s, 0, :, at], (rhs, plane))
        ybuf[0, pl.ds(pl.multiple_of(s * rhs, 8), rhs), :] = low
        ybuf[1, pl.ds(pl.multiple_of(s * rhs, 8), rhs), :] = high
        return carry

    slots = kap_ref.shape[0]
    kappa_rows = pl.ds(cap * rhs, slots)

    faces = {0: (ybuf, yg_ref, ysend, yrecv), 2: (xbuf, xg_ref, xsend, xrecv)}

    def face_copy(base, side, ghost_side):
        axis, index, _ = around[base + side]
        buf, ghost, send, recv = faces[base]
        return pltpu.make_async_remote_copy(
            src_ref=buf.at[side],
            dst_ref=ghost.at[ghost_side],
            send_sem=send.at[side],
            recv_sem=recv.at[ghost_side],
            device_id={axis: index},
            device_id_type=mesh_id,
        )

    def when_near(base, side, action):
        @pl.when(around[base + side][2])
        def _():
            action()

    pl.semaphore_wait(barrier, n_px + n_py - 2)
    for side in range(2):
        when_near(2, side, lambda: face_copy(2, side, 1 - side).start())
    ybuf[0, kappa_rows, :], ybuf[1, kappa_rows, :] = gather_faces(
        lambda at: kap_ref[:, at], (slots, plane)
    )
    lax.fori_loop(0, cap, pack, 0)
    for side in range(2):
        when_near(0, side, lambda: face_copy(0, side, 1 - side).start())
    for base in (0, 2):
        for side in range(2):
            @pl.when(jnp.logical_not(around[base + side][2]))
            def _():
                ghost = faces[base][1]
                ghost[side] = jnp.zeros(ghost.shape[1:], f32)

    for load in loads[cap + 1:]:
        load.wait()
    slot_id = lax.broadcasted_iota(jnp.int32, (slots, 1), 0)
    flips_ref[...] = jnp.where(slot_id < held, 1 - 2 * sgn_ref[...], 0).astype(f32)

    def flips(s, at):
        return flips_ref[pl.ds(s, 1), at]

    def keep(s, part, at, value):
        first_part, rest = split(value)
        cols[s, pl.ds(part * rhs, rhs), at] = first_part
        cols[s, pl.ds((part + 3) * rhs, rhs), at] = rest

    def pair_columns(s, carry):
        for a in range(PS):
            at = pl.ds(a * plane, plane)
            sg = flips(s, at)
            keep(s, 0, at, old_ref[s, 0, :, at] * sg)
            keep(s, 1, at, last_ref[s, 0, :, at] * sg)
        return carry

    lax.fori_loop(0, cap, pair_columns, 0)

    for base in (2, 0):
        for side in range(2):
            when_near(base, side, lambda: face_copy(base, side, 1 - side).wait_send())
            when_near(base, side, lambda: face_copy(base, side, side).wait_recv())

    def rolled(value, glo, ghi, a):
        lo = (plane - a * PS) % plane
        hi = (plane - PS - a * PS) % plane
        blo = jnp.where(
            b_id == 0, pltpu.roll(glo, lo, 1) if lo else glo, pltpu.roll(value, PS, 1)
        )
        bhi = jnp.where(
            b_id == PS - 1,
            pltpu.roll(ghi, hi, 1) if hi else ghi,
            pltpu.roll(value, plane - PS, 1),
        )
        return blo, bhi, pltpu.roll(value, 1, 1), pltpu.roll(value, plane - 1, 1)

    kg_lo, kg_hi = yg_ref[0, kappa_rows, :], yg_ref[1, kappa_rows, :]
    for a in range(PS):
        at = pl.ds(a * plane, plane)
        k = kap_ref[:, at]
        if a == 0:
            below = jnp.where(
                slot_id == 0,
                xg_ref[0, pl.ds(rhs, 1), :],
                pltpu.roll(kap_ref[:, pl.ds(top, plane)], 1, 0),
            )
        else:
            below = kap_ref[:, pl.ds((a - 1) * plane, plane)]
        if a == PS - 1:
            above = jnp.where(
                slot_id == held - 1,
                xg_ref[1, pl.ds(rhs, 1), :],
                pltpu.roll(kap_ref[:, pl.ds(0, plane)], slots - 1, 0),
            )
        else:
            above = kap_ref[:, pl.ds((a + 1) * plane, plane)]
        kr = rolled(k, kg_lo, kg_hi, a)
        ends = (c_id == 0, c_id == PS - 1)
        near = (below, above, kr[0], kr[1]) + tuple(
            jnp.where(end, 0.0, kn) for end, kn in zip(ends, kr[2:])
        )
        weights = [0.5 * (k + kn) for kn in near]
        diag = weights[0]
        for w in weights[1:]:
            diag = diag + w
        weights[4] = jnp.where(ends[0], 0.0, weights[4])
        weights[5] = jnp.where(ends[1], 0.0, weights[5])
        for n, w in enumerate(weights + [diag]):
            weights_ref[n, :, at] = w

    def operate(s, carry):
        live = s < held
        before = jnp.maximum(s - 1, 0)
        after = jnp.minimum(s + 1, cap - 1)
        us = pl.ds(pl.multiple_of(s * rhs, 8), rhs)
        ug_lo, ug_hi = yg_ref[0, us, :], yg_ref[1, us, :]
        for a in range(PS):
            at = pl.ds(a * plane, plane)
            u = last_ref[s, 0, :, at]
            if a == 0:
                low = jnp.where(
                    s == 0, xg_ref[0, pl.ds(0, rhs), :], last_ref[before, 0, :, pl.ds(top, plane)]
                )
            else:
                low = last_ref[s, 0, :, pl.ds((a - 1) * plane, plane)]
            if a == PS - 1:
                high = jnp.where(
                    s == held - 1,
                    xg_ref[1, pl.ds(0, rhs), :],
                    last_ref[after, 0, :, pl.ds(0, plane)],
                )
            else:
                high = last_ref[s, 0, :, pl.ds((a + 1) * plane, plane)]
            near = (low, high) + rolled(u, ug_lo, ug_hi, a)
            image = weights_ref[6, pl.ds(s, 1), at] * u
            for n, un in enumerate(near):
                image = image - weights_ref[n, pl.ds(s, 1), at] * un
            image = jnp.where(live, image, 0.0)
            image_ref[s, 0, :, at] = image
            keep(s, 2, at, image * flips(s, at))
        return carry

    lax.fori_loop(0, cap, operate, 0)

    def one_gram(s, acc):
        whole = cols[s]
        imgs = jnp.concatenate([whole[2 * rhs:3 * rhs], whole[5 * rhs:6 * rhs]], axis=0)
        both = lax.dot_general(
            imgs, whole, (((1,), (1,)), ((), ())), preferred_element_type=f32
        )
        both = both[:, :2 * rhs] + both[:, 3 * rhs:5 * rhs]
        return acc + both[:rhs] + both[rhs:]

    gram_ref[...] = lax.fori_loop(0, cap, one_gram, jnp.zeros((rhs, 2 * rhs), f32))

    def mover(axis, source, slots, send, recv):
        def copy(peer, slot):
            return pltpu.make_async_remote_copy(
                src_ref=source(peer),
                dst_ref=slots.at[slot],
                send_sem=send.at[peer],
                recv_sem=recv.at[slot],
                device_id={axis: peer},
                device_id_type=mesh_id,
            )

        return copy

    def start(copy, me, peers):
        for peer in peers:
            copy(peer, me).start()

    def finish(copy, me, peers):
        for peer in peers:
            copy(peer, peer).wait_recv()
        for peer in peers:
            copy(peer, me).wait_send()

    def total(slots):
        acc = slots[0]
        for p in range(1, slots.shape[0]):
            acc = acc + slots[p]
        return acc

    gram_x_copy = mover("px", lambda p: gram_ref, gram_x, gram_xs, gram_xr)
    gram_y_copy = mover("py", lambda p: gram_y.at[j], gram_y, gram_ys, gram_yr)
    sketch_x_copy = mover("px", lambda p: sketch_ref.at[p], sketch_x, sketch_xs, sketch_xr)
    sketch_y_copy = mover("py", lambda p: sketch_y.at[j], sketch_y, sketch_ys, sketch_yr)
    parts_copy = mover("px", lambda p: parts_x.at[i], parts_x, parts_s, parts_r)

    start(gram_x_copy, i, x_peers)
    gram_x[i] = gram_ref[...]

    cell_bits = cells.bit_length() - 1
    width = sketch_ref.shape[2]
    per = TILE // width
    inner = lax.broadcasted_iota(jnp.int32, (TILE, TILE), 0)
    outer = cells // TILE
    hi_ids = lax.broadcasted_iota(jnp.int32, (outer, TILE), 0)
    tiles = rows_ref.shape[1] // TILE
    scale = 1.0 / math.sqrt(total_cells)

    core = lax.rem(j, 2)
    partner = j + 1 - 2 * core
    half_rows = 3 * rhs // 2

    def tile_of(turn):
        return lax.rem(i // per + 1 + turn, tiles)

    def rows_of(turn):
        return rows_ref[:, pl.ds(pl.multiple_of(tile_of(turn) * TILE, TILE), TILE)]

    def fill(signs_of, turn):
        rows = rows_of(turn)
        inside = parity_sign(jnp.bitwise_and(inner, rows), 8).astype(f32).astype(bf16)
        across = parity_sign(
            jnp.bitwise_and(hi_ids, jnp.right_shift(rows, 8) & (outer - 1)), 4
        ).astype(f32)
        for h in range(outer):
            signs_of[pl.ds(h * TILE, TILE), :] = inside * across[h:h + 1].astype(bf16)

    def spread_of(signs_of):
        flat = cols[...].reshape(cap * 6 * rhs, cells)
        return jnp.dot(flat, signs_of[...], preferred_element_type=f32)

    def core_copy(turn):
        return pltpu.make_async_remote_copy(
            src_ref=core_out.at[turn],
            dst_ref=core_in.at[turn],
            send_sem=core_s.at[turn],
            recv_sem=core_r.at[turn],
            device_id={"py": partner},
            device_id_type=mesh_id,
        )

    def forward(turn):
        core_copy(turn).wait_recv()
        block = core_own[turn] + core_in[turn]
        t = tile_of(turn)
        for r in range(per):
            owner = t * per + r
            sketch_ref[owner] = block[:, r * width:(r + 1) * width]

            @pl.when(owner != i)
            def _():
                sketch_x_copy(owner, i).start()

    def emit(turn, spread):
        rows = rows_of(turn)
        summed = jnp.zeros((3 * rhs, TILE), f32)
        for s in range(cap):
            patch = (offset + s) * n_py + j
            w = parity_sign(
                jnp.bitwise_and(jnp.right_shift(rows, cell_bits), patch), 16
            ).astype(f32)
            base = s * 6 * rhs
            summed = summed + w * (
                spread[base:base + 3 * rhs] + spread[base + 3 * rhs:base + 6 * rhs]
            )
        summed = summed * scale
        core_own[turn] = jnp.where(core == 0, summed[:half_rows], summed[half_rows:])
        core_out[turn] = jnp.where(core == 0, summed[half_rows:], summed[:half_rows])
        core_copy(turn).start()

        @pl.when(turn > 0)
        def _():
            forward(turn - 1)

    def two_tiles(pair_id, carry):
        turn = 2 * pair_id
        fill(table_odd, turn + 1)
        spread = spread_of(table)
        emit(turn, spread)
        fill(table, turn + 2)
        spread = spread_of(table_odd)
        emit(turn + 1, spread)
        return carry

    fill(table, 0)
    lax.fori_loop(0, tiles // 4, two_tiles, 0)
    finish(gram_x_copy, i, x_peers)
    gram_y[j] = total(gram_x)
    start(gram_y_copy, j, y_peers)
    lax.fori_loop(tiles // 4, tiles // 2, two_tiles, 0)
    forward(tiles - 1)
    sketch_x[i] = sketch_ref[i]
    finish(gram_y_copy, j, y_peers)
    proj = total(gram_y) * (1.0 / total_cells)
    finish(sketch_x_copy, i, x_peers)
    sketch_y[j] = total(sketch_x)
    start(sketch_y_copy, j, y_peers)

    proj_head, proj_rest = split(proj)
    none = jnp.zeros((rhs, rhs), bf16)
    both_proj = jnp.concatenate(
        [
            jnp.concatenate([proj_head, none, proj_head, none], axis=1),
            jnp.concatenate([proj_rest, none, jnp.zeros((rhs, 3 * rhs), bf16)], axis=1),
        ],
        axis=0,
    )

    def store_of(s):
        return pltpu.make_async_copy(image_ref.at[s], new_hbm.at[s], out_sem.at[s])

    def one_block(s, carry):
        moved = jnp.dot(both_proj, cols[s], preferred_element_type=f32)
        moved = moved[:rhs] + moved[rhs:]
        image_ref[s, 0] = image_ref[s, 0] - moved * flips(s, pl.ds(0, cells))
        store_of(s).start()
        return carry

    lax.fori_loop(0, cap // 2, one_block, 0)
    finish(sketch_y_copy, j, y_peers)
    halves = []
    for c in range(2):
        acc = sketch_y[c]
        for p in range(c + 2, n_py, 2):
            acc = acc + sketch_y[p]
        halves.append(acc)
    whole = jnp.concatenate(halves, axis=0)
    pair = whole[:2 * rhs]
    second = whole[2 * rhs:]
    images = jnp.concatenate([nn(prev_ref[...], pair), second], axis=0)
    target = tn(resid_ref[...], pair[:rhs])
    parts_x[i] = nt(images, jnp.concatenate([images, target], axis=0))
    start(parts_copy, i, x_peers)
    lax.fori_loop(cap // 2, cap, one_block, 0)
    newer = second - nn(proj, pair)
    share = mine_ref.shape[1]
    chosen = (
        lax.broadcasted_iota(jnp.int32, (width, share), 0)
        == lax.broadcasted_iota(jnp.int32, (width, share), 1) + j * share
    ).astype(f32)
    mine_ref[...] = nn(jnp.concatenate([pair, newer], axis=0), chosen)
    finish(parts_copy, i, x_peers)
    answer_ref[...] = eliminate(total(parts_x))[:, 2 * rhs:].T
    for turn in range(tiles):
        core_copy(turn).wait_send()
    for s in range(cap):
        store_of(s).wait()


def step(n_px, n_py, total_cells, counts, last, old, kap, sgn, rows, prev, resid):
    cap, _, rhs, cells = last.shape
    width = rows.shape[1] // n_px
    plane = PS * PS
    slots = -(-cap // 8) * 8
    yrows = cap * rhs + slots
    tiles = rows.shape[1] // TILE
    half = 3 * rhs // 2
    xrows = rhs + 8
    hbm = pl.BlockSpec(memory_space=pl.ANY)
    sems = lambda n: pltpu.SemaphoreType.DMA((n,))
    return pl.pallas_call(
        functools.partial(step_kernel, n_px, n_py, total_cells),
        out_shape=(
            jax.ShapeDtypeStruct(last.shape, f32),
            jax.ShapeDtypeStruct((3 * rhs, width // n_py), f32),
            jax.ShapeDtypeStruct((rhs, 2 * rhs), f32),
        ),
        in_specs=[SMEM] + [hbm] * 4 + [VMEM] * 3,
        out_specs=(hbm, VMEM, VMEM),
        scratch_shapes=[
            pltpu.VMEM(last.shape, f32),
            pltpu.VMEM(old.shape, f32),
            pltpu.VMEM((slots, cells), f32),
            pltpu.VMEM((slots, cells), jnp.int32),
            sems(2 + 2 * cap), sems(cap),
            pltpu.VMEM((2, xrows, plane), f32),
            pltpu.VMEM((2, yrows, plane), f32),
            pltpu.VMEM((2, xrows, plane), f32),
            pltpu.VMEM((2, yrows, plane), f32),
            sems(2), sems(2), sems(2), sems(2),
            pltpu.VMEM(last.shape, f32),
            pltpu.VMEM((cap, 6 * rhs, cells), bf16),
            pltpu.VMEM((cells, TILE), bf16),
            pltpu.VMEM((rhs, 2 * rhs), f32),
            pltpu.VMEM((n_px, half, width), f32),
            pltpu.VMEM((n_px, rhs, 2 * rhs), f32),
            pltpu.VMEM((n_px, half, width), f32),
            pltpu.VMEM((n_py, rhs, 2 * rhs), f32),
            pltpu.VMEM((n_py, half, width), f32),
            pltpu.VMEM((n_px, 2 * rhs, 3 * rhs), f32),
            sems(n_px), sems(n_px), sems(n_px), sems(n_px),
            sems(n_py), sems(n_py), sems(n_py), sems(n_py),
            sems(n_px), sems(n_px),
            pltpu.VMEM((cells, TILE), bf16),
            pltpu.VMEM((7, slots, cells), f32),
            pltpu.VMEM((slots, cells), f32),
            pltpu.VMEM((tiles, half, TILE), f32),
            pltpu.VMEM((tiles, half, TILE), f32),
            pltpu.VMEM((tiles, half, TILE), f32),
            sems(tiles), sems(tiles),
        ],
        compiler_params=params(collective_id=0, has_side_effects=True),
    )(counts, last, old, kap, sgn, rows, prev, resid)


def body(
    n_px, n_py, counts, coefficient, signs, basis_old, basis_last, residual_factor, previous_coef,
    sample_rows,
):
    total_cells = MEANX * n_px * n_py * coefficient.shape[2]
    rows = sample_rows.reshape(1, -1)
    new_block, mine, answer = step(
        n_px, n_py, total_cells, counts, basis_last, basis_old, coefficient, signs, rows,
        previous_coef.T, residual_factor,
    )
    return (new_block, mine, answer.T)


def solution(mesh):
    in_specs = (
        P(),
        P("px", "py", None),
        P("px", "py", None),
        P("px", "py", None, None),
        P("px", "py", None, None),
        P(),
        P(),
        P(),
    )
    out_specs = (P("px", "py", None, None), P(None, ("px", "py")), P())
    return jax.shard_map(
        functools.partial(body, mesh.shape["px"], mesh.shape["py"]),
        mesh=mesh,
        in_specs=in_specs,
        out_specs=out_specs,
        check_vma=False,
    )
```

```python
import functools
import math

import jax
import jax.numpy as jnp
from jax import lax
from jax.experimental import pallas as pl
from jax.experimental.pallas import tpu as pltpu
from jax.sharding import PartitionSpec as P

PS = 16
MEANX = 2
TILE = 256

highest = lax.Precision.HIGHEST
f32 = jnp.float32
bf16 = jnp.bfloat16
VMEM = pl.BlockSpec(memory_space=pltpu.VMEM)
SMEM = pl.BlockSpec(memory_space=pltpu.SMEM)


def params(**more):
    return pltpu.CompilerParams(vmem_limit_bytes=63 * 1024 * 1024, **more)


def parity_sign(values, bits):
    amount = 1
    while amount < bits:
        amount *= 2
    while amount > 1:
        amount //= 2
        values = jnp.bitwise_xor(values, jnp.right_shift(values, amount))
    return 1 - 2 * jnp.bitwise_and(values, 1)


def split(values):
    head = values.astype(bf16)
    return head, (values - head.astype(f32)).astype(bf16)


def tn(left, right):
    return lax.dot_general(
        left, right, (((0,), (0,)), ((), ())), precision=highest, preferred_element_type=f32
    )


def nt(left, right):
    return lax.dot_general(
        left, right, (((1,), (1,)), ((), ())), precision=highest, preferred_element_type=f32
    )


def eliminate(work):
    size, width = work.shape
    row_id = lax.broadcasted_iota(jnp.int32, (size, 1), 0)
    for step in range(size):
        row = work[step:step + 1, :]
        pivot = row[:, step:step + 1]
        scaled = row / pivot
        column = jnp.where(row_id == step, 0.0, work[:, step:step + 1])
        work = jnp.where(row_id == step, scaled, work - column * scaled)
    return work


def nn(left, right):
    return jnp.dot(left, right, precision=highest, preferred_element_type=f32)


def step_kernel(
    n_px, n_py, total_cells, counts_ref, last_hbm, old_hbm, kap_hbm, sgn_hbm, rows_ref, prev_ref,
    resid_ref, new_hbm, mine_ref, answer_ref, last_ref, old_ref, kap_ref, sgn_ref, in_sem, out_sem,
    xbuf, ybuf, xg_ref, yg_ref, xsend, xrecv, ysend, yrecv, image_ref, cols, table, gram_ref,
    sketch_ref, gram_x, sketch_x, gram_y, sketch_y, parts_x, gram_xs, gram_xr, sketch_xs,
    sketch_xr, gram_ys, gram_yr, sketch_ys, sketch_yr, parts_s, parts_r, weights_ref,
    flips_ref, core_own, core_out, core_in, core_s, core_r,
):
    i = lax.axis_index("px")
    j = lax.axis_index("py")
    cap, _, rhs, cells = last_ref.shape
    plane = PS * PS
    top = (PS - 1) * plane
    mesh_id = pl.DeviceIdType.MESH
    kap_ref[...] = jnp.zeros(kap_ref.shape, f32)
    sgn_ref[...] = jnp.zeros(sgn_ref.shape, jnp.int32)
    pairs = [(last_hbm, last_ref)]
    pairs += [(kap_hbm.at[s], kap_ref.at[pl.ds(s, 1)]) for s in range(cap)]
    pairs += [(old_hbm, old_ref)]
    pairs += [(sgn_hbm.at[s], sgn_ref.at[pl.ds(s, 1)]) for s in range(cap)]
    loads = [
        pltpu.make_async_copy(source, target, in_sem.at[index])
        for index, (source, target) in enumerate(pairs)
    ]
    for load in loads:
        load.start()
    x_peers = [lax.rem(i + d, n_px) for d in range(1, n_px)]
    y_peers = [lax.rem(j + d, n_py) for d in range(1, n_py)]
    barrier = pltpu.get_barrier_semaphore()
    for axis, peers in (("px", x_peers), ("py", y_peers)):
        for peer in peers:
            pl.semaphore_signal(barrier, inc=1, device_id={axis: peer}, device_id_type=mesh_id)
    around = [
        ("py", j - 1, j > 0),
        ("py", j + 1, j < n_py - 1),
        ("px", i - 1, i > 0),
        ("px", i + 1, i < n_px - 1),
    ]
    lane = lax.broadcasted_iota(jnp.int32, (1, plane), 1)
    b_id = lane // PS
    c_id = lane % PS
    held = counts_ref[i]
    offset = jnp.int32(0)
    for t in range(n_px):
        offset = offset + jnp.where(t < i, counts_ref[t], 0)
    tail = jnp.clip(held - 1, 0, cap - 1)

    for load in loads[:cap + 1]:
        load.wait()
    xbuf[0, pl.ds(0, rhs), :] = last_ref[0, 0, :, pl.ds(0, plane)]
    xbuf[0, pl.ds(rhs, 1), :] = kap_ref[pl.ds(0, 1), pl.ds(0, plane)]
    xbuf[1, pl.ds(0, rhs), :] = last_ref[tail, 0, :, pl.ds(top, plane)]
    xbuf[1, pl.ds(rhs, 1), :] = kap_ref[pl.ds(tail, 1), pl.ds(top, plane)]

    def gather_faces(plane_at, shape):
        low = jnp.zeros(shape, f32)
        high = jnp.zeros(shape, f32)
        for a in range(PS):
            value = plane_at(pl.ds(a * plane, plane))
            lo = (a * PS) % plane
            hi = (a * PS + PS) % plane
            low = jnp.where(b_id == a, pltpu.roll(value, lo, 1) if lo else value, low)
            high = jnp.where(b_id == a, pltpu.roll(value, hi, 1) if hi else value, high)
        return low, high

    def pack(s, carry):
        low, high = gather_faces(lambda at: last_ref[s, 0, :, at], (rhs, plane))
        ybuf[0, pl.ds(pl.multiple_of(s * rhs, 8), rhs), :] = low
        ybuf[1, pl.ds(pl.multiple_of(s * rhs, 8), rhs), :] = high
        return carry

    slots = kap_ref.shape[0]
    kappa_rows = pl.ds(cap * rhs, slots)

    faces = {0: (ybuf, yg_ref, ysend, yrecv), 2: (xbuf, xg_ref, xsend, xrecv)}

    def face_copy(base, side, ghost_side):
        axis, index, _ = around[base + side]
        buf, ghost, send, recv = faces[base]
        return pltpu.make_async_remote_copy(
            src_ref=buf.at[side],
            dst_ref=ghost.at[ghost_side],
            send_sem=send.at[side],
            recv_sem=recv.at[ghost_side],
            device_id={axis: index},
            device_id_type=mesh_id,
        )

    def when_near(base, side, action):
        @pl.when(around[base + side][2])
        def _():
            action()

    pl.semaphore_wait(barrier, n_px + n_py - 2)
    for side in range(2):
        when_near(2, side, lambda: face_copy(2, side, 1 - side).start())
    ybuf[0, kappa_rows, :], ybuf[1, kappa_rows, :] = gather_faces(
        lambda at: kap_ref[:, at], (slots, plane)
    )
    lax.fori_loop(0, cap, pack, 0)
    for side in range(2):
        when_near(0, side, lambda: face_copy(0, side, 1 - side).start())
    for base in (0, 2):
        for side in range(2):
            @pl.when(jnp.logical_not(around[base + side][2]))
            def _():
                ghost = faces[base][1]
                ghost[side] = jnp.zeros(ghost.shape[1:], f32)

    for load in loads[cap + 1:]:
        load.wait()
    slot_id = lax.broadcasted_iota(jnp.int32, (slots, 1), 0)
    flips_ref[...] = jnp.where(slot_id < held, 1 - 2 * sgn_ref[...], 0).astype(f32)

    def flips(s, at):
        return flips_ref[pl.ds(s, 1), at]

    def keep(s, part, at, value):
        first_part, rest = split(value)
        cols[s, pl.ds(part * rhs, rhs), at] = first_part
        cols[s, pl.ds((part + 3) * rhs, rhs), at] = rest

    def pair_columns(s, carry):
        for a in range(PS):
            at = pl.ds(a * plane, plane)
            sg = flips(s, at)
            keep(s, 0, at, old_ref[s, 0, :, at] * sg)
            keep(s, 1, at, last_ref[s, 0, :, at] * sg)
        return carry

    lax.fori_loop(0, cap, pair_columns, 0)

    for base in (2, 0):
        for side in range(2):
            when_near(base, side, lambda: face_copy(base, side, 1 - side).wait_send())
            when_near(base, side, lambda: face_copy(base, side, side).wait_recv())

    def rolled(value, glo, ghi, a):
        lo = (plane - a * PS) % plane
        hi = (plane - PS - a * PS) % plane
        blo = jnp.where(
            b_id == 0, pltpu.roll(glo, lo, 1) if lo else glo, pltpu.roll(value, PS, 1)
        )
        bhi = jnp.where(
            b_id == PS - 1,
            pltpu.roll(ghi, hi, 1) if hi else ghi,
            pltpu.roll(value, plane - PS, 1),
        )
        return blo, bhi, pltpu.roll(value, 1, 1), pltpu.roll(value, plane - 1, 1)

    kg_lo, kg_hi = yg_ref[0, kappa_rows, :], yg_ref[1, kappa_rows, :]
    for a in range(PS):
        at = pl.ds(a * plane, plane)
        k = kap_ref[:, at]
        if a == 0:
            below = jnp.where(
                slot_id == 0,
                xg_ref[0, pl.ds(rhs, 1), :],
                pltpu.roll(kap_ref[:, pl.ds(top, plane)], 1, 0),
            )
        else:
            below = kap_ref[:, pl.ds((a - 1) * plane, plane)]
        if a == PS - 1:
            above = jnp.where(
                slot_id == held - 1,
                xg_ref[1, pl.ds(rhs, 1), :],
                pltpu.roll(kap_ref[:, pl.ds(0, plane)], slots - 1, 0),
            )
        else:
            above = kap_ref[:, pl.ds((a + 1) * plane, plane)]
        kr = rolled(k, kg_lo, kg_hi, a)
        ends = (c_id == 0, c_id == PS - 1)
        near = (below, above, kr[0], kr[1]) + tuple(
            jnp.where(end, 0.0, kn) for end, kn in zip(ends, kr[2:])
        )
        weights = [0.5 * (k + kn) for kn in near]
        diag = weights[0]
        for w in weights[1:]:
            diag = diag + w
        weights[4] = jnp.where(ends[0], 0.0, weights[4])
        weights[5] = jnp.where(ends[1], 0.0, weights[5])
        for n, w in enumerate(weights + [diag]):
            weights_ref[n, :, at] = w

    def operate(s, carry):
        live = s < held
        before = jnp.maximum(s - 1, 0)
        after = jnp.minimum(s + 1, cap - 1)
        us = pl.ds(pl.multiple_of(s * rhs, 8), rhs)
        ug_lo, ug_hi = yg_ref[0, us, :], yg_ref[1, us, :]
        for a in range(PS):
            at = pl.ds(a * plane, plane)
            u = last_ref[s, 0, :, at]
            if a == 0:
                low = jnp.where(
                    s == 0, xg_ref[0, pl.ds(0, rhs), :], last_ref[before, 0, :, pl.ds(top, plane)]
                )
            else:
                low = last_ref[s, 0, :, pl.ds((a - 1) * plane, plane)]
            if a == PS - 1:
                high = jnp.where(
                    s == held - 1,
                    xg_ref[1, pl.ds(0, rhs), :],
                    last_ref[after, 0, :, pl.ds(0, plane)],
                )
            else:
                high = last_ref[s, 0, :, pl.ds((a + 1) * plane, plane)]
            near = (low, high) + rolled(u, ug_lo, ug_hi, a)
            image = weights_ref[6, pl.ds(s, 1), at] * u
            for n, un in enumerate(near):
                image = image - weights_ref[n, pl.ds(s, 1), at] * un
            image = jnp.where(live, image, 0.0)
            image_ref[s, 0, :, at] = image
            keep(s, 2, at, image * flips(s, at))
        return carry

    lax.fori_loop(0, cap, operate, 0)

    def one_gram(s, acc):
        whole = cols[s]
        imgs = jnp.concatenate([whole[2 * rhs:3 * rhs], whole[5 * rhs:6 * rhs]], axis=0)
        both = lax.dot_general(
            imgs, whole, (((1,), (1,)), ((), ())), preferred_element_type=f32
        )
        both = both[:, :2 * rhs] + both[:, 3 * rhs:5 * rhs]
        return acc + both[:rhs] + both[rhs:]

    gram_ref[...] = lax.fori_loop(0, cap, one_gram, jnp.zeros((rhs, 2 * rhs), f32))

    def mover(axis, source, slots, send, recv):
        def copy(peer, slot):
            return pltpu.make_async_remote_copy(
                src_ref=source(peer),
                dst_ref=slots.at[slot],
                send_sem=send.at[peer],
                recv_sem=recv.at[slot],
                device_id={axis: peer},
                device_id_type=mesh_id,
            )

        return copy

    def start(copy, me, peers):
        for peer in peers:
            copy(peer, me).start()

    def finish(copy, me, peers):
        for peer in peers:
            copy(peer, peer).wait_recv()
        for peer in peers:
            copy(peer, me).wait_send()

    def total(slots):
        acc = slots[0]
        for p in range(1, slots.shape[0]):
            acc = acc + slots[p]
        return acc

    gram_x_copy = mover("px", lambda p: gram_ref, gram_x, gram_xs, gram_xr)
    gram_y_copy = mover("py", lambda p: gram_y.at[j], gram_y, gram_ys, gram_yr)
    sketch_x_copy = mover("px", lambda p: sketch_ref.at[p], sketch_x, sketch_xs, sketch_xr)
    sketch_y_copy = mover("py", lambda p: sketch_y.at[j], sketch_y, sketch_ys, sketch_yr)
    parts_copy = mover("px", lambda p: parts_x.at[i], parts_x, parts_s, parts_r)

    start(gram_x_copy, i, x_peers)
    gram_x[i] = gram_ref[...]

    cell_bits = cells.bit_length() - 1
    width = sketch_ref.shape[2]
    per = TILE // width
    inner = lax.broadcasted_iota(jnp.int32, (TILE, TILE), 0)
    outer = cells // TILE
    hi_ids = lax.broadcasted_iota(jnp.int32, (outer, TILE), 0)
    tiles = rows_ref.shape[1] // TILE
    scale = 1.0 / math.sqrt(total_cells)

    core = lax.rem(j, 2)
    partner = j + 1 - 2 * core
    half_rows = 3 * rhs // 2

    def tile_of(turn):
        return lax.rem(i // per + 1 + turn, tiles)

    def rows_of(turn):
        return rows_ref[:, pl.ds(pl.multiple_of(tile_of(turn) * TILE, TILE), TILE)]

    def fill(signs_of, turn):
        rows = rows_of(turn)
        inside = parity_sign(jnp.bitwise_and(inner, rows), 8).astype(f32).astype(bf16)
        across = parity_sign(
            jnp.bitwise_and(hi_ids, jnp.right_shift(rows, 8) & (outer - 1)), 4
        ).astype(f32)
        for h in range(outer):
            signs_of[pl.ds(h * TILE, TILE), :] = inside * across[h:h + 1].astype(bf16)

    def spread_of(signs_of):
        flat = cols[...].reshape(cap * 6 * rhs, cells)
        return jnp.dot(flat, signs_of[...], preferred_element_type=f32)

    def core_copy(turn):
        return pltpu.make_async_remote_copy(
            src_ref=core_out.at[turn],
            dst_ref=core_in.at[turn],
            send_sem=core_s.at[turn],
            recv_sem=core_r.at[turn],
            device_id={"py": partner},
            device_id_type=mesh_id,
        )

    def forward(turn):
        core_copy(turn).wait_recv()
        block = core_own[turn] + core_in[turn]
        t = tile_of(turn)
        for r in range(per):
            owner = t * per + r
            sketch_ref[owner] = block[:, r * width:(r + 1) * width]

            @pl.when(owner != i)
            def _():
                sketch_x_copy(owner, i).start()

    def emit(turn, spread):
        rows = rows_of(turn)
        summed = jnp.zeros((3 * rhs, TILE), f32)
        for s in range(cap):
            patch = (offset + s) * n_py + j
            w = parity_sign(
                jnp.bitwise_and(jnp.right_shift(rows, cell_bits), patch), 16
            ).astype(f32)
            base = s * 6 * rhs
            summed = summed + w * (
                spread[base:base + 3 * rhs] + spread[base + 3 * rhs:base + 6 * rhs]
            )
        summed = summed * scale
        core_own[turn] = jnp.where(core == 0, summed[:half_rows], summed[half_rows:])
        core_out[turn] = jnp.where(core == 0, summed[half_rows:], summed[:half_rows])
        core_copy(turn).start()

        @pl.when(turn > 0)
        def _():
            forward(turn - 1)

    def one_tile(turn, carry):
        fill(table, turn)
        emit(turn, spread_of(table))
        return carry

    half = tiles // 2
    lax.fori_loop(0, half, one_tile, 0)
    finish(gram_x_copy, i, x_peers)
    gram_y[j] = total(gram_x)
    start(gram_y_copy, j, y_peers)
    lax.fori_loop(half, tiles, one_tile, 0)
    forward(tiles - 1)
    sketch_x[i] = sketch_ref[i]
    finish(gram_y_copy, j, y_peers)
    proj = total(gram_y) * (1.0 / total_cells)
    finish(sketch_x_copy, i, x_peers)
    sketch_y[j] = total(sketch_x)
    start(sketch_y_copy, j, y_peers)

    proj_head, proj_rest = split(proj)
    none = jnp.zeros((rhs, rhs), bf16)
    both_proj = jnp.concatenate(
        [
            jnp.concatenate([proj_head, none, proj_head, none], axis=1),
            jnp.concatenate([proj_rest, none, jnp.zeros((rhs, 3 * rhs), bf16)], axis=1),
        ],
        axis=0,
    )

    def store_of(s):
        return pltpu.make_async_copy(image_ref.at[s], new_hbm.at[s], out_sem.at[s])

    def one_block(s, carry):
        moved = jnp.dot(both_proj, cols[s], preferred_element_type=f32)
        moved = moved[:rhs] + moved[rhs:]
        image_ref[s, 0] = image_ref[s, 0] - moved * flips(s, pl.ds(0, cells))
        store_of(s).start()
        return carry

    lax.fori_loop(0, cap // 2, one_block, 0)
    finish(sketch_y_copy, j, y_peers)
    halves = []
    for c in range(2):
        acc = sketch_y[c]
        for p in range(c + 2, n_py, 2):
            acc = acc + sketch_y[p]
        halves.append(acc)
    whole = jnp.concatenate(halves, axis=0)
    pair = whole[:2 * rhs]
    second = whole[2 * rhs:]
    images = jnp.concatenate([nn(prev_ref[...], pair), second], axis=0)
    target = tn(resid_ref[...], pair[:rhs])
    parts_x[i] = nt(images, jnp.concatenate([images, target], axis=0))
    start(parts_copy, i, x_peers)
    lax.fori_loop(cap // 2, cap, one_block, 0)
    newer = second - nn(proj, pair)
    share = mine_ref.shape[1]
    chosen = (
        lax.broadcasted_iota(jnp.int32, (width, share), 0)
        == lax.broadcasted_iota(jnp.int32, (width, share), 1) + j * share
    ).astype(f32)
    mine_ref[...] = nn(jnp.concatenate([pair, newer], axis=0), chosen)
    finish(parts_copy, i, x_peers)
    answer_ref[...] = eliminate(total(parts_x))[:, 2 * rhs:].T
    for turn in range(tiles):
        core_copy(turn).wait_send()
    for s in range(cap):
        store_of(s).wait()


def step(n_px, n_py, total_cells, counts, last, old, kap, sgn, rows, prev, resid):
    cap, _, rhs, cells = last.shape
    width = rows.shape[1] // n_px
    plane = PS * PS
    slots = -(-cap // 8) * 8
    yrows = cap * rhs + slots
    tiles = rows.shape[1] // TILE
    half = 3 * rhs // 2
    xrows = rhs + 8
    hbm = pl.BlockSpec(memory_space=pl.ANY)
    sems = lambda n: pltpu.SemaphoreType.DMA((n,))
    return pl.pallas_call(
        functools.partial(step_kernel, n_px, n_py, total_cells),
        out_shape=(
            jax.ShapeDtypeStruct(last.shape, f32),
            jax.ShapeDtypeStruct((3 * rhs, width // n_py), f32),
            jax.ShapeDtypeStruct((rhs, 2 * rhs), f32),
        ),
        in_specs=[SMEM] + [hbm] * 4 + [VMEM] * 3,
        out_specs=(hbm, VMEM, VMEM),
        scratch_shapes=[
            pltpu.VMEM(last.shape, f32),
            pltpu.VMEM(old.shape, f32),
            pltpu.VMEM((slots, cells), f32),
            pltpu.VMEM((slots, cells), jnp.int32),
            sems(2 + 2 * cap), sems(cap),
            pltpu.VMEM((2, xrows, plane), f32),
            pltpu.VMEM((2, yrows, plane), f32),
            pltpu.VMEM((2, xrows, plane), f32),
            pltpu.VMEM((2, yrows, plane), f32),
            sems(2), sems(2), sems(2), sems(2),
            pltpu.VMEM(last.shape, f32),
            pltpu.VMEM((cap, 6 * rhs, cells), bf16),
            pltpu.VMEM((cells, TILE), bf16),
            pltpu.VMEM((rhs, 2 * rhs), f32),
            pltpu.VMEM((n_px, half, width), f32),
            pltpu.VMEM((n_px, rhs, 2 * rhs), f32),
            pltpu.VMEM((n_px, half, width), f32),
            pltpu.VMEM((n_py, rhs, 2 * rhs), f32),
            pltpu.VMEM((n_py, half, width), f32),
            pltpu.VMEM((n_px, 2 * rhs, 3 * rhs), f32),
            sems(n_px), sems(n_px), sems(n_px), sems(n_px),
            sems(n_py), sems(n_py), sems(n_py), sems(n_py),
            sems(n_px), sems(n_px),
            pltpu.VMEM((7, slots, cells), f32),
            pltpu.VMEM((slots, cells), f32),
            pltpu.VMEM((tiles, half, TILE), f32),
            pltpu.VMEM((tiles, half, TILE), f32),
            pltpu.VMEM((tiles, half, TILE), f32),
            sems(tiles), sems(tiles),
        ],
        compiler_params=params(collective_id=0, has_side_effects=True),
    )(counts, last, old, kap, sgn, rows, prev, resid)


def body(
    n_px, n_py, counts, coefficient, signs, basis_old, basis_last, residual_factor, previous_coef,
    sample_rows,
):
    total_cells = MEANX * n_px * n_py * coefficient.shape[2]
    rows = sample_rows.reshape(1, -1)
    new_block, mine, answer = step(
        n_px, n_py, total_cells, counts, basis_last, basis_old, coefficient, signs, rows,
        previous_coef.T, residual_factor,
    )
    return (new_block, mine, answer.T)


def solution(mesh):
    in_specs = (
        P(),
        P("px", "py", None),
        P("px", "py", None),
        P("px", "py", None, None),
        P("px", "py", None, None),
        P(),
        P(),
        P(),
    )
    out_specs = (P("px", "py", None, None), P(None, ("px", "py")), P())
    return jax.shard_map(
        functools.partial(body, mesh.shape["px"], mesh.shape["py"]),
        mesh=mesh,
        in_specs=in_specs,
        out_specs=out_specs,
        check_vma=False,
    )
```

```python
import functools
import math

import jax
import jax.numpy as jnp
from jax import lax
from jax.experimental import pallas as pl
from jax.experimental.pallas import tpu as pltpu
from jax.sharding import PartitionSpec as P

PS = 16
MEANX = 2
TILE = 256

highest = lax.Precision.HIGHEST
f32 = jnp.float32
bf16 = jnp.bfloat16
VMEM = pl.BlockSpec(memory_space=pltpu.VMEM)
SMEM = pl.BlockSpec(memory_space=pltpu.SMEM)


def params(**more):
    return pltpu.CompilerParams(vmem_limit_bytes=63 * 1024 * 1024, **more)


def parity_sign(values, bits):
    amount = 1
    while amount < bits:
        amount *= 2
    while amount > 1:
        amount //= 2
        values = jnp.bitwise_xor(values, jnp.right_shift(values, amount))
    return 1 - 2 * jnp.bitwise_and(values, 1)


def split(values):
    head = values.astype(bf16)
    return head, (values - head.astype(f32)).astype(bf16)


def tn(left, right):
    return lax.dot_general(
        left, right, (((0,), (0,)), ((), ())), precision=highest, preferred_element_type=f32
    )


def nt(left, right):
    return lax.dot_general(
        left, right, (((1,), (1,)), ((), ())), precision=highest, preferred_element_type=f32
    )


def eliminate(work):
    size, width = work.shape
    row_id = lax.broadcasted_iota(jnp.int32, (size, 1), 0)
    for step in range(0, size, 2):
        row0 = work[step:step + 1, :]
        row1 = work[step + 1:step + 2, :]
        col0 = work[:, step:step + 1]
        col1 = work[:, step + 1:step + 2]
        inv0 = 1.0 / row0[:, step:step + 1]
        ratio = row1[:, step:step + 1] * inv0
        left = row0[:, step + 1:step + 2]
        inv1 = 1.0 / (row1[:, step + 1:step + 2] - ratio * left)
        new1 = (row1 - ratio * row0) * inv1
        new0 = (row0 - left * new1) * inv0
        rest = work - col0 * new0 - col1 * new1
        work = jnp.where(row_id == step, new0, jnp.where(row_id == step + 1, new1, rest))
    return work


def nn(left, right):
    return jnp.dot(left, right, precision=highest, preferred_element_type=f32)


def step_kernel(
    n_px, n_py, total_cells, counts_ref, last_hbm, old_hbm, kap_hbm, sgn_hbm, rows_ref, prev_ref,
    resid_ref, new_hbm, mine_ref, answer_ref, last_ref, old_ref, kap_ref, sgn_ref, in_sem, out_sem,
    xbuf, ybuf, xg_ref, yg_ref, xsend, xrecv, ysend, yrecv, image_ref, cols, table, gram_ref,
    sketch_ref, gram_x, sketch_x, gram_y, sketch_y, parts_x, gram_xs, gram_xr, sketch_xs,
    sketch_xr, gram_ys, gram_yr, sketch_ys, sketch_yr, parts_s, parts_r, weights_ref,
    flips_ref, core_own, core_out, core_in, core_s, core_r,
):
    i = lax.axis_index("px")
    j = lax.axis_index("py")
    cap, _, rhs, cells = last_ref.shape
    plane = PS * PS
    top = (PS - 1) * plane
    mesh_id = pl.DeviceIdType.MESH
    kap_ref[...] = jnp.zeros(kap_ref.shape, f32)
    sgn_ref[...] = jnp.zeros(sgn_ref.shape, jnp.int32)
    pairs = [(last_hbm, last_ref)]
    pairs += [(kap_hbm.at[s], kap_ref.at[pl.ds(s, 1)]) for s in range(cap)]
    pairs += [(old_hbm, old_ref)]
    pairs += [(sgn_hbm.at[s], sgn_ref.at[pl.ds(s, 1)]) for s in range(cap)]
    loads = [
        pltpu.make_async_copy(source, target, in_sem.at[index])
        for index, (source, target) in enumerate(pairs)
    ]
    for load in loads:
        load.start()
    x_peers = [lax.rem(i + d, n_px) for d in range(1, n_px)]
    y_peers = [lax.rem(j + d, n_py) for d in range(1, n_py)]
    barrier = pltpu.get_barrier_semaphore()
    for axis, peers in (("px", x_peers), ("py", y_peers)):
        for peer in peers:
            pl.semaphore_signal(barrier, inc=1, device_id={axis: peer}, device_id_type=mesh_id)
    around = [
        ("py", j - 1, j > 0),
        ("py", j + 1, j < n_py - 1),
        ("px", i - 1, i > 0),
        ("px", i + 1, i < n_px - 1),
    ]
    lane = lax.broadcasted_iota(jnp.int32, (1, plane), 1)
    b_id = lane // PS
    c_id = lane % PS
    held = counts_ref[i]
    offset = jnp.int32(0)
    for t in range(n_px):
        offset = offset + jnp.where(t < i, counts_ref[t], 0)
    tail = jnp.clip(held - 1, 0, cap - 1)

    for load in loads[:cap + 1]:
        load.wait()
    xbuf[0, pl.ds(0, rhs), :] = last_ref[0, 0, :, pl.ds(0, plane)]
    xbuf[0, pl.ds(rhs, 1), :] = kap_ref[pl.ds(0, 1), pl.ds(0, plane)]
    xbuf[1, pl.ds(0, rhs), :] = last_ref[tail, 0, :, pl.ds(top, plane)]
    xbuf[1, pl.ds(rhs, 1), :] = kap_ref[pl.ds(tail, 1), pl.ds(top, plane)]

    def gather_faces(plane_at, shape):
        low = jnp.zeros(shape, f32)
        high = jnp.zeros(shape, f32)
        for a in range(PS):
            value = plane_at(pl.ds(a * plane, plane))
            lo = (a * PS) % plane
            hi = (a * PS + PS) % plane
            low = jnp.where(b_id == a, pltpu.roll(value, lo, 1) if lo else value, low)
            high = jnp.where(b_id == a, pltpu.roll(value, hi, 1) if hi else value, high)
        return low, high

    def pack(s, carry):
        low, high = gather_faces(lambda at: last_ref[s, 0, :, at], (rhs, plane))
        ybuf[0, pl.ds(pl.multiple_of(s * rhs, 8), rhs), :] = low
        ybuf[1, pl.ds(pl.multiple_of(s * rhs, 8), rhs), :] = high
        return carry

    slots = kap_ref.shape[0]
    kappa_rows = pl.ds(cap * rhs, slots)

    faces = {0: (ybuf, yg_ref, ysend, yrecv), 2: (xbuf, xg_ref, xsend, xrecv)}

    def face_copy(base, side, ghost_side):
        axis, index, _ = around[base + side]
        buf, ghost, send, recv = faces[base]
        return pltpu.make_async_remote_copy(
            src_ref=buf.at[side],
            dst_ref=ghost.at[ghost_side],
            send_sem=send.at[side],
            recv_sem=recv.at[ghost_side],
            device_id={axis: index},
            device_id_type=mesh_id,
        )

    def when_near(base, side, action):
        @pl.when(around[base + side][2])
        def _():
            action()

    pl.semaphore_wait(barrier, n_px + n_py - 2)
    for side in range(2):
        when_near(2, side, lambda: face_copy(2, side, 1 - side).start())
    ybuf[0, kappa_rows, :], ybuf[1, kappa_rows, :] = gather_faces(
        lambda at: kap_ref[:, at], (slots, plane)
    )
    lax.fori_loop(0, cap, pack, 0)
    for side in range(2):
        when_near(0, side, lambda: face_copy(0, side, 1 - side).start())
    for base in (0, 2):
        for side in range(2):
            @pl.when(jnp.logical_not(around[base + side][2]))
            def _():
                ghost = faces[base][1]
                ghost[side] = jnp.zeros(ghost.shape[1:], f32)

    for load in loads[cap + 1:]:
        load.wait()
    slot_id = lax.broadcasted_iota(jnp.int32, (slots, 1), 0)
    flips_ref[...] = jnp.where(slot_id < held, 1 - 2 * sgn_ref[...], 0).astype(f32)

    def flips(s, at):
        return flips_ref[pl.ds(s, 1), at]

    def keep(s, part, at, value):
        first_part, rest = split(value)
        cols[s, pl.ds(part * rhs, rhs), at] = first_part
        cols[s, pl.ds((part + 3) * rhs, rhs), at] = rest

    chunk = 4 * plane
    chunks = cells // chunk

    def pair_columns(index, carry):
        s = index // chunks
        at = pl.ds(pl.multiple_of(lax.rem(index, chunks) * chunk, chunk), chunk)
        sg = flips(s, at)
        keep(s, 0, at, old_ref[s, 0, :, at] * sg)
        keep(s, 1, at, last_ref[s, 0, :, at] * sg)
        return carry

    lax.fori_loop(0, cap * chunks, pair_columns, 0)

    for base in (2, 0):
        for side in range(2):
            when_near(base, side, lambda: face_copy(base, side, 1 - side).wait_send())
            when_near(base, side, lambda: face_copy(base, side, side).wait_recv())

    def rolled(value, glo, ghi, a):
        lo = (plane - a * PS) % plane
        hi = (plane - PS - a * PS) % plane
        blo = jnp.where(
            b_id == 0, pltpu.roll(glo, lo, 1) if lo else glo, pltpu.roll(value, PS, 1)
        )
        bhi = jnp.where(
            b_id == PS - 1,
            pltpu.roll(ghi, hi, 1) if hi else ghi,
            pltpu.roll(value, plane - PS, 1),
        )
        return blo, bhi, pltpu.roll(value, 1, 1), pltpu.roll(value, plane - 1, 1)

    kg_lo, kg_hi = yg_ref[0, kappa_rows, :], yg_ref[1, kappa_rows, :]
    for a in range(PS):
        at = pl.ds(a * plane, plane)
        k = kap_ref[:, at]
        if a == 0:
            below = jnp.where(
                slot_id == 0,
                xg_ref[0, pl.ds(rhs, 1), :],
                pltpu.roll(kap_ref[:, pl.ds(top, plane)], 1, 0),
            )
        else:
            below = kap_ref[:, pl.ds((a - 1) * plane, plane)]
        if a == PS - 1:
            above = jnp.where(
                slot_id == held - 1,
                xg_ref[1, pl.ds(rhs, 1), :],
                pltpu.roll(kap_ref[:, pl.ds(0, plane)], slots - 1, 0),
            )
        else:
            above = kap_ref[:, pl.ds((a + 1) * plane, plane)]
        kr = rolled(k, kg_lo, kg_hi, a)
        ends = (c_id == 0, c_id == PS - 1)
        near = (below, above, kr[0], kr[1]) + tuple(
            jnp.where(end, 0.0, kn) for end, kn in zip(ends, kr[2:])
        )
        weights = [0.5 * (k + kn) for kn in near]
        diag = weights[0]
        for w in weights[1:]:
            diag = diag + w
        weights[4] = jnp.where(ends[0], 0.0, weights[4])
        weights[5] = jnp.where(ends[1], 0.0, weights[5])
        for n, w in enumerate(weights + [diag]):
            weights_ref[n, :, at] = w

    def operate(s, carry):
        live = s < held
        before = jnp.maximum(s - 1, 0)
        after = jnp.minimum(s + 1, cap - 1)
        us = pl.ds(pl.multiple_of(s * rhs, 8), rhs)
        ug_lo, ug_hi = yg_ref[0, us, :], yg_ref[1, us, :]
        for a in range(PS):
            at = pl.ds(a * plane, plane)
            u = last_ref[s, 0, :, at]
            if a == 0:
                low = jnp.where(
                    s == 0, xg_ref[0, pl.ds(0, rhs), :], last_ref[before, 0, :, pl.ds(top, plane)]
                )
            else:
                low = last_ref[s, 0, :, pl.ds((a - 1) * plane, plane)]
            if a == PS - 1:
                high = jnp.where(
                    s == held - 1,
                    xg_ref[1, pl.ds(0, rhs), :],
                    last_ref[after, 0, :, pl.ds(0, plane)],
                )
            else:
                high = last_ref[s, 0, :, pl.ds((a + 1) * plane, plane)]
            near = (low, high) + rolled(u, ug_lo, ug_hi, a)
            image = weights_ref[6, pl.ds(s, 1), at] * u
            for n, un in enumerate(near):
                image = image - weights_ref[n, pl.ds(s, 1), at] * un
            image = jnp.where(live, image, 0.0)
            image_ref[s, 0, :, at] = image
            keep(s, 2, at, image * flips(s, at))
        return carry

    lax.fori_loop(0, cap, operate, 0)

    def one_gram(s, acc):
        whole = cols[s]
        imgs = jnp.concatenate([whole[2 * rhs:3 * rhs], whole[5 * rhs:6 * rhs]], axis=0)
        both = lax.dot_general(
            imgs, whole, (((1,), (1,)), ((), ())), preferred_element_type=f32
        )
        both = both[:, :2 * rhs] + both[:, 3 * rhs:5 * rhs]
        return acc + both[:rhs] + both[rhs:]

    gram_ref[...] = lax.fori_loop(0, cap, one_gram, jnp.zeros((rhs, 2 * rhs), f32))

    def mover(axis, source, slots, send, recv):
        def copy(peer, slot):
            return pltpu.make_async_remote_copy(
                src_ref=source(peer),
                dst_ref=slots.at[slot],
                send_sem=send.at[peer],
                recv_sem=recv.at[slot],
                device_id={axis: peer},
                device_id_type=mesh_id,
            )

        return copy

    def start(copy, me, peers):
        for peer in peers:
            copy(peer, me).start()

    def finish(copy, me, peers):
        for peer in peers:
            copy(peer, peer).wait_recv()
        for peer in peers:
            copy(peer, me).wait_send()

    def total(slots):
        acc = slots[0]
        for p in range(1, slots.shape[0]):
            acc = acc + slots[p]
        return acc

    gram_x_copy = mover("px", lambda p: gram_ref, gram_x, gram_xs, gram_xr)
    gram_y_copy = mover("py", lambda p: gram_y.at[j], gram_y, gram_ys, gram_yr)
    sketch_x_copy = mover("px", lambda p: sketch_ref.at[p], sketch_x, sketch_xs, sketch_xr)
    sketch_y_copy = mover("py", lambda p: sketch_y.at[j], sketch_y, sketch_ys, sketch_yr)
    parts_copy = mover("px", lambda p: parts_x.at[i], parts_x, parts_s, parts_r)

    start(gram_x_copy, i, x_peers)
    gram_x[i] = gram_ref[...]

    cell_bits = cells.bit_length() - 1
    width = sketch_ref.shape[2]
    per = TILE // width
    inner = lax.broadcasted_iota(jnp.int32, (TILE, TILE), 0)
    outer = cells // TILE
    hi_ids = lax.broadcasted_iota(jnp.int32, (outer, TILE), 0)
    tiles = rows_ref.shape[1] // TILE
    scale = 1.0 / math.sqrt(total_cells)

    core = lax.rem(j, 2)
    partner = j + 1 - 2 * core
    half_rows = 3 * rhs // 2

    def tile_of(turn):
        return lax.rem(i // per + 1 + turn, tiles)

    def rows_of(turn):
        return rows_ref[:, pl.ds(pl.multiple_of(tile_of(turn) * TILE, TILE), TILE)]

    def fill(signs_of, turn):
        rows = rows_of(turn)
        inside = parity_sign(jnp.bitwise_and(inner, rows), 8).astype(f32).astype(bf16)
        across = parity_sign(
            jnp.bitwise_and(hi_ids, jnp.right_shift(rows, 8) & (outer - 1)), 4
        ).astype(f32)
        for h in range(outer):
            signs_of[pl.ds(h * TILE, TILE), :] = inside * across[h:h + 1].astype(bf16)

    def spread_of(signs_of):
        flat = cols[...].reshape(cap * 6 * rhs, cells)
        return jnp.dot(flat, signs_of[...], preferred_element_type=f32)

    def core_copy(turn):
        return pltpu.make_async_remote_copy(
            src_ref=core_out.at[turn],
            dst_ref=core_in.at[turn],
            send_sem=core_s.at[turn],
            recv_sem=core_r.at[turn],
            device_id={"py": partner},
            device_id_type=mesh_id,
        )

    def forward(turn):
        core_copy(turn).wait_recv()
        block = core_own[turn] + core_in[turn]
        t = tile_of(turn)
        for r in range(per):
            owner = t * per + r
            sketch_ref[owner] = block[:, r * width:(r + 1) * width]

            @pl.when(owner != i)
            def _():
                sketch_x_copy(owner, i).start()

    def emit(turn, spread):
        rows = rows_of(turn)
        summed = jnp.zeros((3 * rhs, TILE), f32)
        for s in range(cap):
            patch = (offset + s) * n_py + j
            w = parity_sign(
                jnp.bitwise_and(jnp.right_shift(rows, cell_bits), patch), 16
            ).astype(f32)
            base = s * 6 * rhs
            summed = summed + w * (
                spread[base:base + 3 * rhs] + spread[base + 3 * rhs:base + 6 * rhs]
            )
        summed = summed * scale
        core_own[turn] = jnp.where(core == 0, summed[:half_rows], summed[half_rows:])
        core_out[turn] = jnp.where(core == 0, summed[half_rows:], summed[:half_rows])
        core_copy(turn).start()

        @pl.when(turn > 0)
        def _():
            forward(turn - 1)

    def one_tile(turn, carry):
        fill(table, turn)
        emit(turn, spread_of(table))
        return carry

    half = tiles // 2
    lax.fori_loop(0, half, one_tile, 0)
    finish(gram_x_copy, i, x_peers)
    gram_y[j] = total(gram_x)
    start(gram_y_copy, j, y_peers)
    lax.fori_loop(half, tiles, one_tile, 0)
    forward(tiles - 1)
    sketch_x[i] = sketch_ref[i]
    finish(gram_y_copy, j, y_peers)
    proj = total(gram_y) * (1.0 / total_cells)
    finish(sketch_x_copy, i, x_peers)
    sketch_y[j] = total(sketch_x)
    start(sketch_y_copy, j, y_peers)

    proj_head, proj_rest = split(proj)
    none = jnp.zeros((rhs, rhs), bf16)
    both_proj = jnp.concatenate(
        [
            jnp.concatenate([proj_head, none, proj_head, none], axis=1),
            jnp.concatenate([proj_rest, none, jnp.zeros((rhs, 3 * rhs), bf16)], axis=1),
        ],
        axis=0,
    )

    def store_of(s):
        return pltpu.make_async_copy(image_ref.at[s], new_hbm.at[s], out_sem.at[s])

    def one_block(s, carry):
        moved = jnp.dot(both_proj, cols[s], preferred_element_type=f32)
        moved = moved[:rhs] + moved[rhs:]
        image_ref[s, 0] = image_ref[s, 0] - moved * flips(s, pl.ds(0, cells))
        store_of(s).start()
        return carry

    lax.fori_loop(0, cap // 2, one_block, 0)
    finish(sketch_y_copy, j, y_peers)
    halves = []
    for c in range(2):
        acc = sketch_y[c]
        for p in range(c + 2, n_py, 2):
            acc = acc + sketch_y[p]
        halves.append(acc)
    whole = jnp.concatenate(halves, axis=0)
    pair = whole[:2 * rhs]
    second = whole[2 * rhs:]
    images = jnp.concatenate([nn(prev_ref[...], pair), second], axis=0)
    target = tn(resid_ref[...], pair[:rhs])
    parts_x[i] = nt(images, jnp.concatenate([images, target], axis=0))
    start(parts_copy, i, x_peers)
    lax.fori_loop(cap // 2, cap, one_block, 0)
    newer = second - nn(proj, pair)
    share = mine_ref.shape[1]
    chosen = (
        lax.broadcasted_iota(jnp.int32, (width, share), 0)
        == lax.broadcasted_iota(jnp.int32, (width, share), 1) + j * share
    ).astype(f32)
    mine_ref[...] = nn(jnp.concatenate([pair, newer], axis=0), chosen)
    finish(parts_copy, i, x_peers)
    answer_ref[...] = eliminate(total(parts_x))[:, 2 * rhs:].T
    for turn in range(tiles):
        core_copy(turn).wait_send()
    for s in range(cap):
        store_of(s).wait()


def step(n_px, n_py, total_cells, counts, last, old, kap, sgn, rows, prev, resid):
    cap, _, rhs, cells = last.shape
    width = rows.shape[1] // n_px
    plane = PS * PS
    slots = -(-cap // 8) * 8
    yrows = cap * rhs + slots
    tiles = rows.shape[1] // TILE
    half = 3 * rhs // 2
    xrows = rhs + 8
    hbm = pl.BlockSpec(memory_space=pl.ANY)
    sems = lambda n: pltpu.SemaphoreType.DMA((n,))
    return pl.pallas_call(
        functools.partial(step_kernel, n_px, n_py, total_cells),
        out_shape=(
            jax.ShapeDtypeStruct(last.shape, f32),
            jax.ShapeDtypeStruct((3 * rhs, width // n_py), f32),
            jax.ShapeDtypeStruct((rhs, 2 * rhs), f32),
        ),
        in_specs=[SMEM] + [hbm] * 4 + [VMEM] * 3,
        out_specs=(hbm, VMEM, VMEM),
        scratch_shapes=[
            pltpu.VMEM(last.shape, f32),
            pltpu.VMEM(old.shape, f32),
            pltpu.VMEM((slots, cells), f32),
            pltpu.VMEM((slots, cells), jnp.int32),
            sems(2 + 2 * cap), sems(cap),
            pltpu.VMEM((2, xrows, plane), f32),
            pltpu.VMEM((2, yrows, plane), f32),
            pltpu.VMEM((2, xrows, plane), f32),
            pltpu.VMEM((2, yrows, plane), f32),
            sems(2), sems(2), sems(2), sems(2),
            pltpu.VMEM(last.shape, f32),
            pltpu.VMEM((cap, 6 * rhs, cells), bf16),
            pltpu.VMEM((cells, TILE), bf16),
            pltpu.VMEM((rhs, 2 * rhs), f32),
            pltpu.VMEM((n_px, half, width), f32),
            pltpu.VMEM((n_px, rhs, 2 * rhs), f32),
            pltpu.VMEM((n_px, half, width), f32),
            pltpu.VMEM((n_py, rhs, 2 * rhs), f32),
            pltpu.VMEM((n_py, half, width), f32),
            pltpu.VMEM((n_px, 2 * rhs, 3 * rhs), f32),
            sems(n_px), sems(n_px), sems(n_px), sems(n_px),
            sems(n_py), sems(n_py), sems(n_py), sems(n_py),
            sems(n_px), sems(n_px),
            pltpu.VMEM((7, slots, cells), f32),
            pltpu.VMEM((slots, cells), f32),
            pltpu.VMEM((tiles, half, TILE), f32),
            pltpu.VMEM((tiles, half, TILE), f32),
            pltpu.VMEM((tiles, half, TILE), f32),
            sems(tiles), sems(tiles),
        ],
        compiler_params=params(collective_id=0, has_side_effects=True),
    )(counts, last, old, kap, sgn, rows, prev, resid)


def place_kernel(new_ref, mine_ref, answer_ref, new_out, mine_out, answer_out, sems):
    cap = new_ref.shape[0]
    moves = [(mine_ref, mine_out), (answer_ref, answer_out)]
    moves += [(new_ref.at[s], new_out.at[s]) for s in range(cap)]
    copies = [
        pltpu.make_async_copy(source, target, sems.at[n])
        for n, (source, target) in enumerate(moves)
    ]
    for copy in copies:
        copy.start()
    for copy in copies:
        copy.wait()


def place(*arrays):
    hbm = pl.BlockSpec(memory_space=pl.ANY)
    return pl.pallas_call(
        place_kernel,
        out_shape=tuple(jax.ShapeDtypeStruct(a.shape, f32) for a in arrays),
        in_specs=[hbm] * 3,
        out_specs=(hbm,) * 3,
        scratch_shapes=[pltpu.SemaphoreType.DMA((2 + arrays[0].shape[0],))],
        compiler_params=params(),
    )(*arrays)


def body(
    n_px, n_py, counts, coefficient, signs, basis_old, basis_last, residual_factor, previous_coef,
    sample_rows,
):
    total_cells = MEANX * n_px * n_py * coefficient.shape[2]
    rows = sample_rows.reshape(1, -1)
    new_block, mine, answer = step(
        n_px, n_py, total_cells, counts, basis_last, basis_old, coefficient, signs, rows,
        previous_coef.T, residual_factor,
    )
    new_block, mine, answer = place(new_block, mine, answer)
    return (new_block, mine, answer.T)


def solution(mesh):
    in_specs = (
        P(),
        P("px", "py", None),
        P("px", "py", None),
        P("px", "py", None, None),
        P("px", "py", None, None),
        P(),
        P(),
        P(),
    )
    out_specs = (P("px", "py", None, None), P(None, ("px", "py")), P())
    return jax.shard_map(
        functools.partial(body, mesh.shape["px"], mesh.shape["py"]),
        mesh=mesh,
        in_specs=in_specs,
        out_specs=out_specs,
        check_vma=False,
    )
```
